256 devices in a mesh: col: 64 (over z, y, core), row: 4 (over x).
Axes of the slice: x: 4, y: 4, z: 8, core: 2. Of those that a mesh axis runs over, the one named last changes fastest.
Arguments:
- right_side: float32 [8192, 256], P(('row', 'col')), may hold values from -6 to 6
- prior_solution: bfloat16 [131072, 256], P('col'), may hold values from -6 to 6
- factor_codes: bfloat16 [8192, 131072], P('row', 'col'), may hold values from -0.015625 to 0.015625
- block_scale: float32 [4, 512], P('row', 'col'), may hold values from 0.3 to 3
- diag_inverse: bfloat16 [4, 2048, 2048], P('row', 'col'), may hold values from -0.125 to 0.125
- inner_factor: bfloat16 [4, 4, 2048, 2048], P('row', None, 'col'), may hold values from -0.125 to 0.125
Outputs:
- solved: float32 [8192, 256], P(('row', 'col'))
The draws below stay inside these ranges and needn't reach their ends.
All inputs are finite; a program needn't handle non-finite values.
Results may differ from the reference program's by a relative error of at most 0.0095.
Values may be sent and summed in bfloat16 or wider, within the bound.
A program may use at most 64 MiB of HBM per device.

```python
import math
import jax
import jax.numpy as jnp
from jax import lax

PB = 2048
KB = 256
RHS = 256
PANELS = 4
K = 131072


def levels(rng, shape, cuts, smallest, high):
    gain = 1.0
    for position, blocks in cuts:
        steps = jax.random.uniform(jax.random.fold_in(jax.random.fold_in(rng, 6), position), (blocks,), jnp.float32, smallest / len(cuts), high / len(cuts))
        gain = gain * jnp.repeat(jnp.exp(steps), shape[position] // blocks).reshape((-1,) + (1,) * (len(shape) - 1 - position))
    return gain


def normal_values(stream_key, extent, deviation, reach, split=(), kind=jnp.bfloat16):
    drawn = deviation * jax.random.normal(stream_key, extent, jnp.float32)
    if split:
        drawn = drawn * levels(stream_key, extent, split, -0.22, 0.18)
    return jnp.clip(drawn, -reach, reach).astype(kind)


def setup_inputs(seed: int = 0) -> dict:
    streams_of = jax.random.split(jax.random.key(seed), 7)
    right_side = normal_values(streams_of[0], (PANELS * PB, RHS), 1.0, 6.0, ((0, 256),), jnp.float32)
    prior_solution = normal_values(streams_of[1], (K, RHS), 1.0, 6.0, ((0, 64),))
    factor_codes = normal_values(streams_of[2], (PANELS * PB, K), K ** -0.5, 0.015625, ((0, 4), (1, 64)))
    block_scale = jnp.clip(jnp.exp(math.log(3.0) - 2.3025851 * jax.random.uniform(streams_of[3], (PANELS, K // KB), jnp.float32) ** levels(streams_of[3], (PANELS, K // KB), ((0, 4), (1, 64)), -0.2, 0.2)), 0.3, 3.0)
    diag_inverse = normal_values(streams_of[4], (PANELS, PB, PB), PB ** -0.5, 0.125, ((0, 4), (1, 64)))
    inner_factor = normal_values(streams_of[5], (PANELS, PANELS, PB, PB), PB ** -0.5, 0.125, ((0, 4), (2, 64)))
    return dict(right_side=right_side, prior_solution=prior_solution, factor_codes=factor_codes, block_scale=block_scale, diag_inverse=diag_inverse, inner_factor=inner_factor)


def reference(right_side, prior_solution, factor_codes, block_scale, diag_inverse, inner_factor):
    panels = block_scale.shape[0]
    blocks_all = block_scale.shape[1]
    block_cols = factor_codes.shape[1] // blocks_all
    panel_rows = factor_codes.shape[0] // panels
    scale_rows = jnp.repeat(block_scale, panel_rows, axis=0)

    def add_block(summed, column_block):
        first = (column_block * block_cols).astype(jnp.int32)
        coded = lax.dynamic_slice_in_dim(factor_codes, first, block_cols, 1)
        earlier = lax.dynamic_slice_in_dim(prior_solution, first, block_cols, 0)
        scaling = lax.dynamic_slice_in_dim(scale_rows, column_block.astype(jnp.int32), 1, 1)
        return summed + scaling * jnp.dot(coded, earlier, preferred_element_type=jnp.float32), None

    initial = jnp.zeros((factor_codes.shape[0], prior_solution.shape[1]), jnp.float32)
    prior_term, _ = lax.scan(add_block, initial, jnp.arange(blocks_all, dtype=jnp.int32))
    rhs = right_side - prior_term
    outputs = []
    rounded_list = []
    for panel_index in range(panels):
        current = rhs[panel_index * panel_rows:(panel_index + 1) * panel_rows]
        for earlier_index in range(panel_index):
            current = current - jnp.dot(inner_factor[panel_index, earlier_index], rounded_list[earlier_index], preferred_element_type=jnp.float32)
        result = jnp.dot(diag_inverse[panel_index], current.astype(jnp.bfloat16), preferred_element_type=jnp.float32)
        outputs.append(result)
        rounded_list.append(result.astype(jnp.bfloat16))
    return jnp.concatenate(outputs, axis=0)
```

```python
import functools

import jax
import jax.numpy as jnp
from jax import lax
from jax.experimental import pallas as pl
from jax.experimental.pallas import tpu as pltpu
from jax.sharding import PartitionSpec as P

MESH = pl.DeviceIdType.MESH
F32, BF16 = jnp.float32, jnp.bfloat16


def dot_t(a, b):
    return lax.dot_general(a, b, (((1,), (1,)), ((), ())), preferred_element_type=F32)


def kernel(
    np_, nz, ny,
    right_ref, prior_ref, codes_ref, scale_ref, diag_ref, inner_ref, out_ref,
    right_v, prior_v, codes_v, prior_t, place, pt, core_out, core_in, half_sum, y_out, y_in, z_out, z_in,
    w, act, x_out, res, final_out, final_in,
    in_sem, codes_sem, w_sem, wy_s, wy_r, wc_s, wc_r, c_s, c_r, y_s, y_r, z_s, z_r, a_s, a_r, x_s, f_s, f_r,
):
    p, j = lax.axis_index("row"), lax.axis_index("col")
    group = ny * 2
    z, g = j // group, j % group
    y, c = g // 2, g % 2
    rows = right_ref.shape[0]
    blocks = scale_ref.shape[1]
    kb = prior_ref.shape[0] // blocks
    row_block = rows * group
    half = right_ref.shape[1] // 2
    chunk = half // ny

    def col_of(z_, y_, c_):
        return z_ * group + y_ * 2 + c_

    def remote(src, dst, send, recv, row, col):
        return pltpu.make_async_remote_copy(
            src_ref=src, dst_ref=dst, send_sem=send, recv_sem=recv, device_id={"row": row, "col": col}, device_id_type=MESH
        )

    barrier = pltpu.get_barrier_semaphore()

    def greet(row, col):
        pl.semaphore_signal(barrier, inc=1, device_id={"row": row, "col": col}, device_id_type=MESH)

    greet(p, col_of(z, y, 1 - c))

    @pl.loop(1, ny)
    def _(d):
        greet(p, col_of(z, (y + d) % ny, c))
        greet(p, col_of(z, (y + d) % ny, 1 - c))

    @pl.loop(1, nz)
    def _(d):
        greet(p, col_of((z + d) % nz, y, c))

    @pl.loop(1, np_)
    def _(d):
        @pl.loop(0, nz)
        def _(zz):
            greet((p + d) % np_, col_of(zz, y, c))

    load_prior = pltpu.make_async_copy(prior_ref, prior_v, in_sem.at[0])
    load_right = pltpu.make_async_copy(right_ref, right_v, in_sem.at[1])
    load_prior.start()
    load_right.start()

    def load_codes(i):
        zb = (z + 1 + i) % nz
        return pltpu.make_async_copy(
            codes_ref.at[pl.ds(pl.multiple_of(zb * row_block, row_block), row_block)], codes_v.at[i], codes_sem.at[i]
        )

    @pl.loop(0, nz)
    def _(i):
        load_codes(i).start()

    def load_inner(m):
        return pltpu.make_async_copy(inner_ref.at[0, m], w.at[m, g], w_sem.at[m])

    load_diag = pltpu.make_async_copy(diag_ref.at[0], w.at[p, g], w_sem.at[p])

    @pl.loop(0, p)
    def _(m):
        load_inner(m).start()

    load_diag.start()

    load_prior.wait()
    for b in range(blocks):
        part = prior_v[b * kb : (b + 1) * kb, :].astype(F32) * scale_ref[0, b]
        prior_t[:, b * kb : (b + 1) * kb] = part.T.astype(BF16)
    load_right.wait()
    place[...] = jnp.zeros_like(place)
    place[pl.ds(pl.multiple_of(g * rows, rows), rows), :] = right_v[...]

    pl.semaphore_wait(barrier, 1 + 2 * (ny - 1) + (nz - 1) + (np_ - 1) * nz)

    def w_y(m, d):
        to = (y + d) % ny
        return remote(w.at[m, g], w.at[m, g], wy_s.at[m, d], wy_r.at[m, y], p, col_of(z, to, c))

    def w_y_arrival(m, d):
        src = (y + d) % ny
        slot = src * 2 + c
        return remote(w.at[m, slot], w.at[m, slot], wy_s.at[m, d], wy_r.at[m, src], p, col_of(z, src, c))

    def w_c(m, yy):
        slot = yy * 2 + c
        return remote(w.at[m, slot], w.at[m, slot], wc_s.at[m, yy], wc_r.at[m, yy], p, col_of(z, y, 1 - c))

    def w_c_arrival(m, yy):
        slot = yy * 2 + 1 - c
        return remote(w.at[m, slot], w.at[m, slot], wc_s.at[m, yy], wc_r.at[m, yy], p, col_of(z, y, 1 - c))

    load_diag.wait()

    @pl.loop(0, p)
    def _(m):
        load_inner(m).wait()

    @pl.loop(0, p + 1)
    def _(m):
        @pl.loop(1, ny)
        def _(d):
            w_y(m, d).start()

        w_c(m, y).start()

    def forward(m):
        @pl.loop(1, ny)
        def _(d):
            w_y_arrival(m, d).wait_recv()
            w_c(m, (y + d) % ny).start()

    def core_copy(i):
        return remote(core_out.at[i], core_in.at[i], c_s.at[i], c_r.at[i], p, col_of(z, y, 1 - c))

    def y_copy(i, d):
        to = (y + d) % ny
        return remote(y_out.at[i, to], y_in.at[i, y], y_s.at[i, d], y_r.at[i, y], p, col_of(z, to, c))

    def y_arrival(i, d):
        src = (y + d) % ny
        return remote(y_out.at[i, src], y_in.at[i, src], y_s.at[i, d], y_r.at[i, src], p, col_of(z, src, c))

    def z_copy(i):
        to = (z + 1 + i) % nz
        return remote(z_out.at[i], z_in.at[z], z_s.at[i], z_r.at[z], p, col_of(to, y, c))

    def z_arrival(d):
        src = (z + d) % nz
        return remote(z_out.at[0], z_in.at[src], z_s.at[0], z_r.at[src], p, col_of(src, y, c))

    def across_y(i):
        core_copy(i).wait_recv()
        total = half_sum[i].reshape(half, row_block) + core_in[i].astype(F32)
        total = total.reshape(ny, chunk, row_block)
        half_sum[i] = total
        y_out[i] = total.astype(BF16)

        @pl.loop(1, ny)
        def _(d):
            y_copy(i, d).start()

    def across_z(i):
        total = half_sum[i, y]
        for d in range(1, ny):
            y_arrival(i, d).wait_recv()
            total = total + y_in[i, (y + d) % ny].astype(F32)
        return total

    lag = min(2, nz - 1)

    @pl.loop(0, nz)
    def _(i):
        load_codes(i).wait()
        pt[...] = dot_t(prior_t[...], codes_v[i]).reshape(2, half, row_block)

        @pl.when(i == nz - 1)
        def _():
            pt[...] -= place[...].T.reshape(2, half, row_block)

        core_out[i] = pt[1 - c].astype(BF16)
        core_copy(i).start()
        half_sum[i] = pt[c].reshape(ny, chunk, row_block)

        @pl.when(i >= lag)
        def _():
            across_y(i - lag)

    @pl.loop(nz - lag, nz)
    def _(i):
        across_y(i)

    forward(0)

    @pl.loop(0, nz - 1)
    def _(i):
        z_out[i] = across_z(i).astype(BF16)
        z_copy(i).start()

    own = across_z(nz - 1)
    for d in range(1, nz):
        z_arrival(d).wait_recv()
        own = own + z_in[(z + d) % nz].astype(F32)
    res[...] = -own

    def times(s, skip_own):
        @pl.loop(0, ny)
        def _(yy):
            w_c_arrival(s, yy).wait_recv()

        total = jnp.zeros((chunk, row_block), F32)
        for d in range(nz):
            src = (z + d) % nz
            if not (skip_own and d == 0):
                remote(x_out, act.at[s, src], x_s.at[0, 0], a_r.at[s, src], p, col_of(src, y, c)).wait_recv()
            columns = pl.ds(pl.multiple_of(src * row_block, row_block), row_block)
            total = total + dot_t(act[s, src], w[s, :, :, columns].reshape(row_block, row_block))
        return total

    @pl.loop(0, p)
    def _(s):
        forward(s + 1)
        res[...] -= times(s, False)

    act[p, z] = res[...].astype(BF16)

    def a_copy(d):
        to = (z + d) % nz
        return remote(act.at[p, z], act.at[p, z], a_s.at[d], a_r.at[p, z], p, col_of(to, y, c))

    @pl.loop(1, nz)
    def _(d):
        a_copy(d).start()

    solved = times(p, True)
    x_out[...] = solved.astype(BF16)

    def x_copy(q, d):
        to = (z + d) % nz
        return remote(x_out, act.at[p, z], x_s.at[q, d], a_r.at[p, z], q, col_of(to, y, c))

    @pl.loop(p + 1, np_)
    def _(q):
        @pl.loop(0, nz)
        def _(d):
            x_copy(q, d).start()

    place[:half, :row_block] = jnp.zeros((half, row_block), F32)
    place[pl.ds(pl.multiple_of(y * chunk, chunk), chunk), :row_block] = solved
    final_out[...] = place[:half, :row_block].T.reshape(group, rows, half)

    def f_copy(d):
        to = (g + d) % group
        return remote(final_out.at[to], final_in.at[g], f_s.at[d], f_r.at[g], p, z * group + to)

    def f_arrival(d):
        src = (g + d) % group
        return remote(final_out.at[src], final_in.at[src], f_s.at[d], f_r.at[src], p, z * group + src)

    @pl.loop(1, group)
    def _(d):
        f_copy(d).start()

    final_in[g] = final_out[g]

    @pl.loop(1, group)
    def _(d):
        f_arrival(d).wait_recv()

    for cc in range(2):
        total = final_in[cc]
        for yy in range(1, ny):
            total = total + final_in[yy * 2 + cc]
        out_ref[:, cc * half : (cc + 1) * half] = total

    @pl.loop(0, p + 1)
    def _(m):
        @pl.loop(1, ny)
        def _(d):
            w_y(m, d).wait_send()

        @pl.loop(0, ny)
        def _(yy):
            w_c(m, yy).wait_send()

    @pl.loop(0, nz)
    def _(i):
        core_copy(i).wait_send()

        @pl.loop(1, ny)
        def _(d):
            y_copy(i, d).wait_send()

    @pl.loop(0, nz - 1)
    def _(i):
        z_copy(i).wait_send()
        a_copy(i + 1).wait_send()

    @pl.loop(p + 1, np_)
    def _(q):
        @pl.loop(0, nz)
        def _(d):
            x_copy(q, d).wait_send()

    @pl.loop(1, group)
    def _(d):
        f_copy(d).wait_send()


def local(np_, nz, ny, right_side, prior_solution, factor_codes, block_scale, diag_inverse, inner_factor):
    rows, rhs = right_side.shape
    depth = prior_solution.shape[0]
    group = ny * 2
    row_block = rows * group
    half = rhs // 2
    chunk = half // ny
    width = diag_inverse.shape[-1]
    dma = pltpu.SemaphoreType.DMA
    scratch = [
        pltpu.VMEM((rows, rhs), F32),
        pltpu.VMEM((depth, rhs), BF16),
        pltpu.VMEM((nz, row_block, depth), BF16),
        pltpu.VMEM((rhs, depth), BF16),
        pltpu.VMEM((row_block, rhs), F32),
        pltpu.VMEM((2, half, row_block), F32),
        pltpu.VMEM((nz, half, row_block), BF16),
        pltpu.VMEM((nz, half, row_block), BF16),
        pltpu.VMEM((nz, ny, chunk, row_block), F32),
        pltpu.VMEM((nz, ny, chunk, row_block), BF16),
        pltpu.VMEM((nz, ny, chunk, row_block), BF16),
        pltpu.VMEM((nz, chunk, row_block), BF16),
        pltpu.VMEM((nz, chunk, row_block), BF16),
        pltpu.VMEM((np_, group, rows, width), BF16),
        pltpu.VMEM((np_, nz, chunk, row_block), BF16),
        pltpu.VMEM((chunk, row_block), BF16),
        pltpu.VMEM((chunk, row_block), F32),
        pltpu.VMEM((group, rows, half), F32),
        pltpu.VMEM((group, rows, half), F32),
        dma((2,)),
        dma((nz,)),
        dma((np_,)),
        dma((np_, ny)),
        dma((np_, ny)),
        dma((np_, ny)),
        dma((np_, ny)),
        dma((nz,)),
        dma((nz,)),
        dma((nz, ny)),
        dma((nz, ny)),
        dma((nz,)),
        dma((nz,)),
        dma((nz,)),
        dma((np_, nz)),
        dma((np_, nz)),
        dma((group,)),
        dma((group,)),
    ]
    anywhere = pl.BlockSpec(memory_space=pl.ANY)
    return pl.pallas_call(
        functools.partial(kernel, np_, nz, ny),
        out_shape=jax.ShapeDtypeStruct((rows, rhs), F32),
        in_specs=[anywhere, anywhere, anywhere, pl.BlockSpec(memory_space=pltpu.SMEM), anywhere, anywhere],
        out_specs=pl.BlockSpec(memory_space=pltpu.VMEM),
        scratch_shapes=scratch,
        compiler_params=pltpu.CompilerParams(collective_id=0, has_side_effects=True, vmem_limit_bytes=48 * 2**20),
        cost_estimate=pl.CostEstimate(
            flops=2 * nz * row_block * depth * rhs, bytes_accessed=2 * nz * row_block * depth, transcendentals=0
        ),
    )(right_side, prior_solution, factor_codes, block_scale, diag_inverse, inner_factor)


def build(mesh, ny):
    np_ = mesh.shape["row"]
    nz = mesh.shape["col"] // (2 * ny)
    return jax.shard_map(
        functools.partial(local, np_, nz, ny),
        mesh=mesh,
        in_specs=(
            P(("row", "col"), None),
            P("col", None),
            P("row", "col"),
            P("row", "col"),
            P("row", "col", None),
            P("row", None, "col", None),
        ),
        out_specs=P(("row", "col"), None),
        check_vma=False,
    )


def solution(mesh):
    return build(mesh, 4)
```

```python
import functools

import jax
import jax.numpy as jnp
from jax import lax
from jax.experimental import pallas as pl
from jax.experimental.pallas import tpu as pltpu
from jax.sharding import PartitionSpec as P

MESH = pl.DeviceIdType.MESH
F32, BF16 = jnp.float32, jnp.bfloat16


def dot_t(a, b):
    return lax.dot_general(a, b, (((1,), (1,)), ((), ())), preferred_element_type=F32)


def kernel(
    np_, nz, ny,
    right_ref, prior_ref, codes_ref, scale_ref, diag_ref, inner_ref, out_ref,
    right_v, prior_v, codes_v, prior_t, place, pt, core_out, core_in, half_sum, y_out, y_in, z_out, z_in,
    w, lcol, macc, mw, act, x_out, res, final_out, final_in,
    in_sem, codes_sem, w_sem, wy_s, wy_r, wc_s, wc_r, la_s, la_r, l_s, l_r, my_s, my_r, mc_s, mc_r, c_s, c_r, y_s, y_r, z_s, z_r, a_s, a_r, x_s, f_s, f_r,
):
    p, j = lax.axis_index("row"), lax.axis_index("col")
    group = ny * 2
    z, g = j // group, j % group
    y, c = g // 2, g % 2
    rows = right_ref.shape[0]
    blocks = scale_ref.shape[1]
    kb = prior_ref.shape[0] // blocks
    row_block = rows * group
    half = right_ref.shape[1] // 2
    chunk = half // ny
    last = jnp.maximum(p - 1, 0)
    far_first = sorted(range(nz), key=lambda d: -min(d, nz - d))

    def col_of(z_, y_, c_):
        return z_ * group + y_ * 2 + c_

    def remote(src, dst, send, recv, row, col):
        return pltpu.make_async_remote_copy(
            src_ref=src, dst_ref=dst, send_sem=send, recv_sem=recv, device_id={"row": row, "col": col}, device_id_type=MESH
        )

    barrier = pltpu.get_barrier_semaphore()

    def greet(row, col):
        pl.semaphore_signal(barrier, inc=1, device_id={"row": row, "col": col}, device_id_type=MESH)

    greet(p, col_of(z, y, 1 - c))

    @pl.loop(1, ny)
    def _(d):
        greet(p, col_of(z, (y + d) % ny, c))
        greet(p, col_of(z, (y + d) % ny, 1 - c))

    @pl.loop(1, nz)
    def _(d):
        greet(p, col_of((z + d) % nz, y, c))

    @pl.loop(1, np_)
    def _(d):
        @pl.loop(0, nz)
        def _(zz):
            greet((p + d) % np_, col_of(zz, y, c))

    load_prior = pltpu.make_async_copy(prior_ref, prior_v, in_sem.at[0])
    load_right = pltpu.make_async_copy(right_ref, right_v, in_sem.at[1])
    load_prior.start()
    load_right.start()

    def load_codes(i):
        zb = (z + 1 + i) % nz
        return pltpu.make_async_copy(
            codes_ref.at[pl.ds(pl.multiple_of(zb * row_block, row_block), row_block)], codes_v.at[i], codes_sem.at[i]
        )

    @pl.loop(0, nz)
    def _(i):
        load_codes(i).start()

    def load_inner(m):
        return pltpu.make_async_copy(inner_ref.at[0, m], w.at[m, g], w_sem.at[m])

    load_diag = pltpu.make_async_copy(diag_ref.at[0], w.at[p, g], w_sem.at[p])

    @pl.loop(0, p)
    def _(m):
        load_inner(m).start()

    load_diag.start()

    load_prior.wait()
    for b in range(blocks):
        part = prior_v[b * kb : (b + 1) * kb, :].astype(F32) * scale_ref[0, b]
        prior_t[:, b * kb : (b + 1) * kb] = part.T.astype(BF16)
    load_right.wait()
    place[...] = jnp.zeros_like(place)
    place[pl.ds(pl.multiple_of(g * rows, rows), rows), :] = right_v[...]

    pl.semaphore_wait(barrier, 1 + 2 * (ny - 1) + (nz - 1) + (np_ - 1) * nz)

    def w_y(m, d):
        to = (y + d) % ny
        return remote(w.at[m, g], w.at[m, g], wy_s.at[m, d], wy_r.at[m, y], p, col_of(z, to, c))

    def w_y_arrival(m, d):
        src = (y + d) % ny
        slot = src * 2 + c
        return remote(w.at[m, slot], w.at[m, slot], wy_s.at[m, d], wy_r.at[m, src], p, col_of(z, src, c))

    def w_c(m, yy):
        slot = yy * 2 + c
        return remote(w.at[m, slot], w.at[m, slot], wc_s.at[m, yy], wc_r.at[m, yy], p, col_of(z, y, 1 - c))

    def w_c_arrival(m, yy):
        slot = yy * 2 + 1 - c
        return remote(w.at[m, slot], w.at[m, slot], wc_s.at[m, yy], wc_r.at[m, yy], p, col_of(z, y, 1 - c))

    load_diag.wait()

    @pl.loop(0, p)
    def _(m):
        load_inner(m).wait()

    def share(m):
        @pl.loop(1, ny)
        def _(d):
            w_y(m, d).start()

        w_c(m, y).start()

    def gathered(m):
        @pl.loop(0, ny)
        def _(yy):
            w_c_arrival(m, yy).wait_recv()

    def forward(m):
        @pl.loop(1, ny)
        def _(d):
            w_y_arrival(m, d).wait_recv()
            w_c(m, (y + d) % ny).start()

    own_columns = pl.ds(pl.multiple_of(g * row_block, row_block), row_block)

    def la_copy(d):
        to = (g + d) % group
        columns = pl.ds(pl.multiple_of(to * row_block, row_block), row_block)
        return remote(w.at[last, g, :, columns], lcol.at[z, g], la_s.at[d], la_r.at[g], p, z * group + to)

    def la_arrival(d):
        src = (g + d) % group
        return remote(lcol.at[z, src], lcol.at[z, src], la_s.at[d], la_r.at[src], p, z * group + src)

    far = nz // 2

    def l_half(owner, h):
        return lcol.at[owner, pl.ds(pl.multiple_of(h * (group // 2), group // 2), group // 2)]

    def l_move(k, h, way):
        step = 1 - 2 * way
        owner = (z + nz - (k - 1) * step) % nz
        to = (z + nz + step) % nz
        part = l_half(owner, h)
        return remote(part, part, l_s.at[way, k - 1, h], l_r.at[owner, h], p, col_of(to, y, c))

    def l_arrival(off, h):
        owner = (z + off) % nz
        part = l_half(owner, h)
        return remote(part, part, l_s.at[0, 0, h], l_r.at[owner, h], p, col_of((z + 1) % nz, y, c))

    def l_start(h):
        l_move(1, h, 0).start()
        if far > 1:
            l_move(1, h, 1).start()

    def l_pass(k, h):
        l_arrival(nz - k, h).wait_recv()
        l_move(k + 1, h, 0).start()

        @pl.when(k < far - 1)
        def _():
            l_arrival(k, h).wait_recv()
            l_move(k + 1, h, 1).start()

    @pl.when(p > 0)
    def _():
        @pl.loop(1, group)
        def _(d):
            la_copy(d).start()

        lcol[z, g] = w[last, g, :, own_columns]

    share(p)

    def m_y(d):
        to = (y + d) % ny
        return remote(mw.at[g], mw.at[g], my_s.at[d], my_r.at[y], p, col_of(z, to, c))

    def m_y_arrival(d):
        src = (y + d) % ny
        slot = src * 2 + c
        return remote(mw.at[slot], mw.at[slot], my_s.at[d], my_r.at[src], p, col_of(z, src, c))

    def m_c(yy):
        slot = yy * 2 + c
        return remote(mw.at[slot], mw.at[slot], mc_s.at[yy], mc_r.at[yy], p, col_of(z, y, 1 - c))

    def m_c_arrival(yy):
        slot = yy * 2 + 1 - c
        return remote(mw.at[slot], mw.at[slot], mc_s.at[yy], mc_r.at[yy], p, col_of(z, y, 1 - c))

    def core_copy(i):
        return remote(core_out.at[i], core_in.at[i], c_s.at[i], c_r.at[i], p, col_of(z, y, 1 - c))

    def y_copy(i, d):
        to = (y + d) % ny
        return remote(y_out.at[i, to], y_in.at[i, y], y_s.at[i, d], y_r.at[i, y], p, col_of(z, to, c))

    def y_arrival(i, d):
        src = (y + d) % ny
        return remote(y_out.at[i, src], y_in.at[i, src], y_s.at[i, d], y_r.at[i, src], p, col_of(z, src, c))

    def z_copy(i):
        to = (z + 1 + i) % nz
        return remote(z_out.at[i], z_in.at[z], z_s.at[i], z_r.at[z], p, col_of(to, y, c))

    def z_arrival(d):
        src = (z + d) % nz
        return remote(z_out.at[0], z_in.at[src], z_s.at[0], z_r.at[src], p, col_of(src, y, c))

    def across_y(i):
        core_copy(i).wait_recv()
        total = half_sum[i].reshape(half, row_block) + core_in[i].astype(F32)
        total = total.reshape(ny, chunk, row_block)
        half_sum[i] = total
        y_out[i] = total.astype(BF16)

        @pl.loop(1, ny)
        def _(d):
            y_copy(i, d).start()

    def across_z(i):
        total = half_sum[i, y]
        for d in range(1, ny):
            y_arrival(i, d).wait_recv()
            total = total + y_in[i, (y + d) % ny].astype(F32)
        return total

    lag = min(2, nz - 1)

    @pl.loop(0, nz)
    def _(i):
        load_codes(i).wait()
        pt[...] = dot_t(prior_t[...], codes_v[i]).reshape(2, half, row_block)

        @pl.when(i == nz - 1)
        def _():
            pt[...] -= place[...].T.reshape(2, half, row_block)

        core_out[i] = pt[1 - c].astype(BF16)
        core_copy(i).start()
        half_sum[i] = pt[c].reshape(ny, chunk, row_block)

        @pl.when(i >= lag)
        def _():
            across_y(i - lag)

        @pl.when((i == nz // 2) & (p > 0))
        def _():
            @pl.loop(1, group)
            def _(d):
                la_arrival(d).wait_recv()

            @pl.loop(0, 2)
            def _(h):
                l_start(h)

    @pl.loop(nz - lag, nz)
    def _(i):
        across_y(i)

    @pl.loop(0, p - 1)
    def _(m):
        share(m)

    @pl.when(p == 0)
    def _():
        forward(p)

    @pl.loop(0, nz - 1)
    def _(i):
        z_out[i] = across_z(i).astype(BF16)
        z_copy(i).start()

        @pl.when((p > 0) & (i < 2 * far - 2))
        def _():
            l_pass(1 + i // 2, i % 2)

    @pl.when(p > 0)
    def _():
        forward(p)

    own = across_z(nz - 1)
    for d in range(1, nz):
        z_arrival(d).wait_recv()
        own = own + z_in[(z + d) % nz].astype(F32)
    res[...] = -own

    def a_copy(d):
        to = (z + d) % nz
        return remote(act.at[p, z], act.at[p, z], a_s.at[d], a_r.at[p, z], p, col_of(to, y, c))

    def send_current():
        act[p, z] = res[...].astype(BF16)

        for d in far_first[:-1]:
            a_copy(d).start()

    def act_arrival(s, src):
        return remote(x_out, act.at[s, src], x_s.at[0, 0], a_r.at[s, src], p, col_of(src, y, c))

    def times(s, own_here):
        total = jnp.zeros((chunk, row_block), F32)
        for d in range(nz):
            src = (z + d) % nz
            if not (own_here and d == 0):
                act_arrival(s, src).wait_recv()
            columns = pl.ds(pl.multiple_of(src * row_block, row_block), row_block)
            total = total + dot_t(act[s, src], w[s, :, :, columns].reshape(row_block, row_block))
        return total

    @pl.when(p <= 1)
    def _():
        send_current()

    @pl.when(p > 0)
    def _():
        gathered(p)

        @pl.loop(0, p - 1)
        def _(m):
            forward(m)

        def columns_of(d):
            return pl.ds(pl.multiple_of(((z + d) % nz) * row_block, row_block), row_block)

        def part(d, block):
            return jnp.dot(
                w[p, :, :, columns_of(d)].reshape(row_block, row_block),
                block.reshape(row_block, row_block),
                preferred_element_type=F32,
            )

        macc[...] = jnp.zeros_like(macc)

        @pl.loop(1, nz + 1)
        def _(t):
            off = (t + far) % nz

            @pl.when((off == far) | ((off == far - 1) & (off > 0)))
            def _():
                @pl.loop(0, 2)
                def _(h):
                    l_arrival(off, h).wait_recv()

            macc[...] += part(off, lcol[(z + off) % nz])

        mw[g] = macc[...].astype(BF16)

        @pl.loop(1, ny)
        def _(d):
            m_y(d).start()

        m_c(y).start()

        @pl.loop(1, ny)
        def _(d):
            m_y_arrival(d).wait_recv()
            m_c((y + d) % ny).start()

        @pl.loop(0, p - 1)
        def _(s):
            gathered(s)
            res[...] -= times(s, False)

    @pl.when(p > 1)
    def _():
        send_current()

    @pl.when(p == 0)
    def _():
        gathered(p)

    res[...] = times(p, True)

    @pl.when(p > 0)
    def _():
        @pl.loop(0, ny)
        def _(yy):
            m_c_arrival(yy).wait_recv()

        total = jnp.zeros((chunk, row_block), F32)
        for src in range(nz):
            act_arrival(last, src).wait_recv()
            total = total + dot_t(act[last, src], mw[src])
        res[...] -= total

    solved = res[...]
    x_out[...] = solved.astype(BF16)

    def x_copy(q, d):
        to = (z + d) % nz
        return remote(x_out, act.at[p, z], x_s.at[q, d], a_r.at[p, z], q, col_of(to, y, c))

    @pl.loop(p + 1, np_)
    def _(q):
        for d in far_first:
            x_copy(q, d).start()

    place[:half, :row_block] = jnp.zeros((half, row_block), F32)
    place[pl.ds(pl.multiple_of(y * chunk, chunk), chunk), :row_block] = solved
    final_out[...] = place[:half, :row_block].T.reshape(group, rows, half)

    def f_copy(d):
        to = (g + d) % group
        return remote(final_out.at[to], final_in.at[g], f_s.at[d], f_r.at[g], p, z * group + to)

    def f_arrival(d):
        src = (g + d) % group
        return remote(final_out.at[src], final_in.at[src], f_s.at[d], f_r.at[src], p, z * group + src)

    @pl.loop(1, group)
    def _(d):
        f_copy(d).start()

    final_in[g] = final_out[g]

    @pl.loop(1, group)
    def _(d):
        f_arrival(d).wait_recv()

    for cc in range(2):
        total = final_in[cc]
        for yy in range(1, ny):
            total = total + final_in[yy * 2 + cc]
        out_ref[:, cc * half : (cc + 1) * half] = total

    def shared(m):
        @pl.loop(1, ny)
        def _(d):
            w_y(m, d).wait_send()

        @pl.loop(0, ny)
        def _(yy):
            w_c(m, yy).wait_send()

    shared(p)

    @pl.loop(0, p - 1)
    def _(m):
        shared(m)

    @pl.when(p > 0)
    def _():
        @pl.loop(1, group)
        def _(d):
            la_copy(d).wait_send()

        @pl.loop(0, 2)
        def _(h):
            @pl.loop(1, far + 1)
            def _(k):
                l_move(k, h, 0).wait_send()

            @pl.loop(1, far)
            def _(k):
                l_move(k, h, 1).wait_send()

        @pl.loop(1, ny)
        def _(d):
            m_y(d).wait_send()

        @pl.loop(0, ny)
        def _(yy):
            m_c(yy).wait_send()

    @pl.loop(0, nz)
    def _(i):
        core_copy(i).wait_send()

        @pl.loop(1, ny)
        def _(d):
            y_copy(i, d).wait_send()

    @pl.loop(0, nz - 1)
    def _(i):
        z_copy(i).wait_send()
        a_copy(i + 1).wait_send()

    @pl.loop(p + 1, np_)
    def _(q):
        @pl.loop(0, nz)
        def _(d):
            x_copy(q, d).wait_send()

    @pl.loop(1, group)
    def _(d):
        f_copy(d).wait_send()


def local(np_, nz, ny, right_side, prior_solution, factor_codes, block_scale, diag_inverse, inner_factor):
    rows, rhs = right_side.shape
    depth = prior_solution.shape[0]
    group = ny * 2
    row_block = rows * group
    half = rhs // 2
    chunk = half // ny
    width = diag_inverse.shape[-1]
    dma = pltpu.SemaphoreType.DMA
    scratch = [
        pltpu.VMEM((rows, rhs), F32),
        pltpu.VMEM((depth, rhs), BF16),
        pltpu.VMEM((nz, row_block, depth), BF16),
        pltpu.VMEM((rhs, depth), BF16),
        pltpu.VMEM((row_block, rhs), F32),
        pltpu.VMEM((2, half, row_block), F32),
        pltpu.VMEM((nz, half, row_block), BF16),
        pltpu.VMEM((nz, half, row_block), BF16),
        pltpu.VMEM((nz, ny, chunk, row_block), F32),
        pltpu.VMEM((nz, ny, chunk, row_block), BF16),
        pltpu.VMEM((nz, ny, chunk, row_block), BF16),
        pltpu.VMEM((nz, chunk, row_block), BF16),
        pltpu.VMEM((nz, chunk, row_block), BF16),
        pltpu.VMEM((np_, group, rows, width), BF16),
        pltpu.VMEM((nz, group, rows, row_block), BF16),
        pltpu.VMEM((row_block, row_block), F32),
        pltpu.VMEM((group, row_block, row_block), BF16),
        pltpu.VMEM((np_, nz, chunk, row_block), BF16),
        pltpu.VMEM((chunk, row_block), BF16),
        pltpu.VMEM((chunk, row_block), F32),
        pltpu.VMEM((group, rows, half), F32),
        pltpu.VMEM((group, rows, half), F32),
        dma((2,)),
        dma((nz,)),
        dma((np_,)),
        dma((np_, ny)),
        dma((np_, ny)),
        dma((np_, ny)),
        dma((np_, ny)),
        dma((group,)),
        dma((group,)),
        dma((2, nz // 2, 2)),
        dma((nz, 2)),
        dma((ny,)),
        dma((ny,)),
        dma((ny,)),
        dma((ny,)),
        dma((nz,)),
        dma((nz,)),
        dma((nz, ny)),
        dma((nz, ny)),
        dma((nz,)),
        dma((nz,)),
        dma((nz,)),
        dma((np_, nz)),
        dma((np_, nz)),
        dma((group,)),
        dma((group,)),
    ]
    anywhere = pl.BlockSpec(memory_space=pl.ANY)
    return pl.pallas_call(
        functools.partial(kernel, np_, nz, ny),
        out_shape=jax.ShapeDtypeStruct((rows, rhs), F32),
        in_specs=[anywhere, anywhere, anywhere, pl.BlockSpec(memory_space=pltpu.SMEM), anywhere, anywhere],
        out_specs=pl.BlockSpec(memory_space=pltpu.VMEM),
        scratch_shapes=scratch,
        compiler_params=pltpu.CompilerParams(collective_id=0, has_side_effects=True, vmem_limit_bytes=60 * 2**20),
        cost_estimate=pl.CostEstimate(
            flops=2 * nz * row_block * depth * rhs, bytes_accessed=2 * nz * row_block * depth, transcendentals=0
        ),
    )(right_side, prior_solution, factor_codes, block_scale, diag_inverse, inner_factor)


def build(mesh, ny):
    np_ = mesh.shape["row"]
    nz = mesh.shape["col"] // (2 * ny)
    return jax.shard_map(
        functools.partial(local, np_, nz, ny),
        mesh=mesh,
        in_specs=(
            P(("row", "col"), None),
            P("col", None),
            P("row", "col"),
            P("row", "col"),
            P("row", "col", None),
            P("row", None, "col", None),
        ),
        out_specs=P(("row", "col"), None),
        check_vma=False,
    )


def solution(mesh):
    return build(mesh, 4)
```

```python
import functools

import jax
import jax.numpy as jnp
from jax import lax
from jax.experimental import pallas as pl
from jax.experimental.pallas import tpu as pltpu
from jax.sharding import PartitionSpec as P

MESH = pl.DeviceIdType.MESH
F32, BF16 = jnp.float32, jnp.bfloat16


def dot_t(a, b):
    return lax.dot_general(a, b, (((1,), (1,)), ((), ())), preferred_element_type=F32)


def kernel(
    np_, nz, ny,
    right_ref, prior_ref, codes_ref, scale_ref, diag_ref, inner_ref, out_ref,
    right_v, prior_v, codes_v, prior_t, place, pt, core_out, core_in, half_sum, y_out, y_in, z_out, z_in,
    w, lcol, macc, mw, act, x_out, res, final_out, final_in,
    in_sem, codes_sem, w_sem, wy_s, wy_r, wc_s, wc_r, la_s, la_r, l_s, l_r, my_s, my_r, mc_s, mc_r, c_s, c_r, y_s, y_r, z_s, z_r, a_s, a_r, x_s, f_s, f_r, ready,
):
    p, j = lax.axis_index("row"), lax.axis_index("col")
    group = ny * 2
    z, g = j // group, j % group
    y, c = g // 2, g % 2
    rows = right_ref.shape[0]
    blocks = scale_ref.shape[1]
    kb = prior_ref.shape[0] // blocks
    row_block = rows * group
    half = right_ref.shape[1] // 2
    chunk = half // ny
    last = jnp.maximum(p - 1, 0)
    far_first = sorted(range(nz), key=lambda d: -min(d, nz - d))

    def col_of(z_, y_, c_):
        return z_ * group + y_ * 2 + c_

    def remote(src, dst, send, recv, row, col):
        return pltpu.make_async_remote_copy(
            src_ref=src, dst_ref=dst, send_sem=send, recv_sem=recv, device_id={"row": row, "col": col}, device_id_type=MESH
        )

    barrier = pltpu.get_barrier_semaphore()

    def greet(row, col):
        pl.semaphore_signal(barrier, inc=1, device_id={"row": row, "col": col}, device_id_type=MESH)

    greet(p, col_of(z, y, 1 - c))

    @pl.loop(1, ny)
    def _(d):
        greet(p, col_of(z, (y + d) % ny, c))
        greet(p, col_of(z, (y + d) % ny, 1 - c))

    @pl.loop(1, nz)
    def _(d):
        greet(p, col_of((z + d) % nz, y, c))

    @pl.loop(1, np_)
    def _(d):
        greet((p + d) % np_, j)

    load_prior = pltpu.make_async_copy(prior_ref, prior_v, in_sem.at[0])
    load_right = pltpu.make_async_copy(right_ref, right_v, in_sem.at[1])
    load_prior.start()
    load_right.start()

    def load_codes(i):
        zb = (z + 1 + i) % nz
        return pltpu.make_async_copy(
            codes_ref.at[pl.ds(pl.multiple_of(zb * row_block, row_block), row_block)], codes_v.at[i], codes_sem.at[i]
        )

    @pl.loop(0, nz)
    def _(i):
        load_codes(i).start()

    def load_inner(m):
        return pltpu.make_async_copy(inner_ref.at[0, m], w.at[m, g], w_sem.at[m])

    load_diag = pltpu.make_async_copy(diag_ref.at[0], w.at[p, g], w_sem.at[p])

    @pl.loop(0, p)
    def _(m):
        load_inner(m).start()

    load_diag.start()

    load_prior.wait()
    for b in range(blocks):
        part = prior_v[b * kb : (b + 1) * kb, :].astype(F32) * scale_ref[0, b]
        prior_t[:, b * kb : (b + 1) * kb] = part.T.astype(BF16)
    load_right.wait()
    place[...] = jnp.zeros_like(place)
    place[pl.ds(pl.multiple_of(g * rows, rows), rows), :] = right_v[...]

    pl.semaphore_wait(barrier, 1 + 2 * (ny - 1) + (nz - 1) + (np_ - 1))

    @pl.loop(0, p)
    def _(q):
        pl.semaphore_signal(ready.at[p], inc=1, device_id={"row": q, "col": j}, device_id_type=MESH)

    def w_y(m, d):
        to = (y + d) % ny
        return remote(w.at[m, g], w.at[m, g], wy_s.at[m, d], wy_r.at[m, y], p, col_of(z, to, c))

    def w_y_arrival(m, d):
        src = (y + d) % ny
        slot = src * 2 + c
        return remote(w.at[m, slot], w.at[m, slot], wy_s.at[m, d], wy_r.at[m, src], p, col_of(z, src, c))

    def w_c(m, yy):
        slot = yy * 2 + c
        return remote(w.at[m, slot], w.at[m, slot], wc_s.at[m, yy], wc_r.at[m, yy], p, col_of(z, y, 1 - c))

    def w_c_arrival(m, yy):
        slot = yy * 2 + 1 - c
        return remote(w.at[m, slot], w.at[m, slot], wc_s.at[m, yy], wc_r.at[m, yy], p, col_of(z, y, 1 - c))

    load_diag.wait()

    @pl.loop(0, p)
    def _(m):
        load_inner(m).wait()

    def share(m):
        @pl.loop(1, ny)
        def _(d):
            w_y(m, d).start()

        w_c(m, y).start()

    def gathered(m):
        @pl.loop(0, ny)
        def _(yy):
            w_c_arrival(m, yy).wait_recv()

    def forward(m):
        @pl.loop(1, ny)
        def _(d):
            w_y_arrival(m, d).wait_recv()
            w_c(m, (y + d) % ny).start()

    own_columns = pl.ds(pl.multiple_of(g * row_block, row_block), row_block)

    def la_copy(d):
        to = (g + d) % group
        columns = pl.ds(pl.multiple_of(to * row_block, row_block), row_block)
        return remote(w.at[last, g, :, columns], lcol.at[z, g], la_s.at[d], la_r.at[g], p, z * group + to)

    def la_arrival(d):
        src = (g + d) % group
        return remote(lcol.at[z, src], lcol.at[z, src], la_s.at[d], la_r.at[src], p, z * group + src)

    far = nz // 2

    def l_half(owner, h):
        return lcol.at[owner, pl.ds(pl.multiple_of(h * (group // 2), group // 2), group // 2)]

    def l_move(k, h, way):
        step = 1 - 2 * way
        owner = (z + nz - (k - 1) * step) % nz
        to = (z + nz + step) % nz
        part = l_half(owner, h)
        return remote(part, part, l_s.at[way, k - 1, h], l_r.at[owner, h], p, col_of(to, y, c))

    def l_arrival(off, h):
        owner = (z + off) % nz
        part = l_half(owner, h)
        return remote(part, part, l_s.at[0, 0, h], l_r.at[owner, h], p, col_of((z + 1) % nz, y, c))

    def l_start(h):
        l_move(1, h, 0).start()
        if far > 1:
            l_move(1, h, 1).start()

    def l_pass(k, h):
        l_arrival(nz - k, h).wait_recv()
        l_move(k + 1, h, 0).start()

        @pl.when(k < far - 1)
        def _():
            l_arrival(k, h).wait_recv()
            l_move(k + 1, h, 1).start()

    @pl.when(p > 0)
    def _():
        @pl.loop(1, group)
        def _(d):
            la_copy(d).start()

        lcol[z, g] = w[last, g, :, own_columns]

    def m_y(d):
        to = (y + d) % ny
        return remote(mw.at[g], mw.at[g], my_s.at[d], my_r.at[y], p, col_of(z, to, c))

    def m_y_arrival(d):
        src = (y + d) % ny
        slot = src * 2 + c
        return remote(mw.at[slot], mw.at[slot], my_s.at[d], my_r.at[src], p, col_of(z, src, c))

    def m_c(yy):
        slot = yy * 2 + c
        return remote(mw.at[slot], mw.at[slot], mc_s.at[yy], mc_r.at[yy], p, col_of(z, y, 1 - c))

    def m_c_arrival(yy):
        slot = yy * 2 + 1 - c
        return remote(mw.at[slot], mw.at[slot], mc_s.at[yy], mc_r.at[yy], p, col_of(z, y, 1 - c))

    def core_copy(i):
        return remote(core_out.at[i], core_in.at[i], c_s.at[i], c_r.at[i], p, col_of(z, y, 1 - c))

    def y_copy(i, d):
        to = (y + d) % ny
        return remote(y_out.at[i, to], y_in.at[i, y], y_s.at[i, d], y_r.at[i, y], p, col_of(z, to, c))

    def y_arrival(i, d):
        src = (y + d) % ny
        return remote(y_out.at[i, src], y_in.at[i, src], y_s.at[i, d], y_r.at[i, src], p, col_of(z, src, c))

    def z_copy(i):
        to = (z + 1 + i) % nz
        return remote(z_out.at[i], z_in.at[z], z_s.at[i], z_r.at[z], p, col_of(to, y, c))

    def z_arrival(d):
        src = (z + d) % nz
        return remote(z_out.at[0], z_in.at[src], z_s.at[0], z_r.at[src], p, col_of(src, y, c))

    def across_y(i):
        core_copy(i).wait_recv()
        total = half_sum[i].reshape(half, row_block) + core_in[i].astype(F32)
        total = total.reshape(ny, chunk, row_block)
        half_sum[i] = total
        y_out[i] = total.astype(BF16)

        @pl.loop(1, ny)
        def _(d):
            y_copy(i, d).start()

    def across_z(i):
        total = half_sum[i, y]
        for d in range(1, ny):
            y_arrival(i, d).wait_recv()
            total = total + y_in[i, (y + d) % ny].astype(F32)
        return total

    lag = min(2, nz - 1)

    @pl.loop(0, nz)
    def _(i):
        load_codes(i).wait()
        pt[...] = dot_t(prior_t[...], codes_v[i]).reshape(2, half, row_block)

        @pl.when(i == nz - 1)
        def _():
            pt[...] -= place[...].T.reshape(2, half, row_block)

        core_out[i] = pt[1 - c].astype(BF16)
        core_copy(i).start()
        half_sum[i] = pt[c].reshape(ny, chunk, row_block)

        @pl.when(i >= lag)
        def _():
            across_y(i - lag)

        @pl.when((i == nz // 2) & (p > 0))
        def _():
            @pl.loop(1, group)
            def _(d):
                la_arrival(d).wait_recv()

            @pl.loop(0, 2)
            def _(h):
                l_start(h)

    @pl.loop(nz - lag, nz)
    def _(i):
        across_y(i)

    share(p)

    def l_pass_both(k):
        if k < far:

            @pl.when(p > 0)
            def _():
                @pl.loop(0, 2)
                def _(h):
                    l_pass(k, h)

    l_pass_both(1)

    @pl.loop(0, nz - 1)
    def _(i):
        z_out[i] = across_z(i).astype(BF16)
        z_copy(i).start()

    @pl.loop(0, p - 1)
    def _(m):
        share(m)

    l_pass_both(2)

    def a_copy(d):
        to = (z + d) % nz
        return remote(act.at[p, z], act.at[p, z], a_s.at[d], a_r.at[p, z], p, col_of(to, y, c))

    def send_current():
        act[p, z] = res[...].astype(BF16)

        for d in far_first[:-1]:
            a_copy(d).start()

    def act_arrival(s, src):
        return remote(x_out, act.at[s, src], x_s.at[0, 0], a_r.at[s, src], p, col_of(src, y, c))

    def times(s, own_here):
        total = jnp.zeros((chunk, row_block), F32)
        for d in range(nz):
            src = (z + d) % nz
            if not (own_here and d == 0):
                act_arrival(s, src).wait_recv()
            columns = pl.ds(pl.multiple_of(src * row_block, row_block), row_block)
            total = total + dot_t(act[s, src], w[s, :, :, columns].reshape(row_block, row_block))
        return total

    for k in range(3, far):
        l_pass_both(k)

    @pl.when(p > 0)
    def _():
        forward(p)
        gathered(p)

        def columns_of(d):
            return pl.ds(pl.multiple_of(((z + d) % nz) * row_block, row_block), row_block)

        def part(d, block):
            return jnp.dot(
                w[p, :, :, columns_of(d)].reshape(row_block, row_block),
                block.reshape(row_block, row_block),
                preferred_element_type=F32,
            )

        macc[...] = jnp.zeros_like(macc)

        @pl.loop(1, nz + 1)
        def _(t):
            off = (t + far) % nz

            @pl.when((off == far) | ((off == far - 1) & (off > 0)))
            def _():
                @pl.loop(0, 2)
                def _(h):
                    l_arrival(off, h).wait_recv()

            macc[...] += part(off, lcol[(z + off) % nz])

        mw[g] = macc[...].astype(BF16)

        @pl.loop(1, ny)
        def _(d):
            m_y(d).start()

        m_c(y).start()

    own = across_z(nz - 1)
    for d in range(1, nz):
        z_arrival(d).wait_recv()
        own = own + z_in[(z + d) % nz].astype(F32)
    res[...] = -own

    @pl.when(p <= 1)
    def _():
        send_current()

    @pl.when(p == 0)
    def _():
        forward(p)

    @pl.when(p > 0)
    def _():
        @pl.loop(0, p - 1)
        def _(m):
            forward(m)

        @pl.loop(1, ny)
        def _(d):
            m_y_arrival(d).wait_recv()
            m_c((y + d) % ny).start()

        @pl.loop(0, p - 1)
        def _(s):
            gathered(s)
            res[...] -= times(s, False)

    @pl.when(p > 1)
    def _():
        send_current()

    @pl.when(p == 0)
    def _():
        gathered(p)

    res[...] = times(p, True)

    @pl.when(p > 0)
    def _():
        @pl.loop(0, ny)
        def _(yy):
            m_c_arrival(yy).wait_recv()

        total = jnp.zeros((chunk, row_block), F32)
        for src in range(nz):
            act_arrival(last, src).wait_recv()
            total = total + dot_t(act[last, src], mw[src])
        res[...] -= total

    solved = res[...]
    x_out[...] = solved.astype(BF16)

    def x_copy(q, d):
        to = (z + d) % nz
        return remote(x_out, act.at[p, z], x_s.at[q, d], a_r.at[p, z], q, col_of(to, y, c))

    @pl.loop(p + 1, np_)
    def _(q):
        pl.semaphore_wait(ready.at[q], 1)
        for d in far_first:
            x_copy(q, d).start()

    place[:half, :row_block] = jnp.zeros((half, row_block), F32)
    place[pl.ds(pl.multiple_of(y * chunk, chunk), chunk), :row_block] = solved
    final_out[...] = place[:half, :row_block].T.reshape(group, rows, half)

    def f_copy(d):
        to = (g + d) % group
        return remote(final_out.at[to], final_in.at[g], f_s.at[d], f_r.at[g], p, z * group + to)

    def f_arrival(d):
        src = (g + d) % group
        return remote(final_out.at[src], final_in.at[src], f_s.at[d], f_r.at[src], p, z * group + src)

    @pl.loop(1, group)
    def _(d):
        f_copy(d).start()

    final_in[g] = final_out[g]

    @pl.loop(1, group)
    def _(d):
        f_arrival(d).wait_recv()

    for cc in range(2):
        total = final_in[cc]
        for yy in range(1, ny):
            total = total + final_in[yy * 2 + cc]
        out_ref[:, cc * half : (cc + 1) * half] = total

    def shared(m):
        @pl.loop(1, ny)
        def _(d):
            w_y(m, d).wait_send()

        @pl.loop(0, ny)
        def _(yy):
            w_c(m, yy).wait_send()

    shared(p)

    @pl.loop(0, p - 1)
    def _(m):
        shared(m)

    @pl.when(p > 0)
    def _():
        @pl.loop(1, group)
        def _(d):
            la_copy(d).wait_send()

        @pl.loop(0, 2)
        def _(h):
            @pl.loop(1, far + 1)
            def _(k):
                l_move(k, h, 0).wait_send()

            @pl.loop(1, far)
            def _(k):
                l_move(k, h, 1).wait_send()

        @pl.loop(1, ny)
        def _(d):
            m_y(d).wait_send()

        @pl.loop(0, ny)
        def _(yy):
            m_c(yy).wait_send()

    @pl.loop(0, nz)
    def _(i):
        core_copy(i).wait_send()

        @pl.loop(1, ny)
        def _(d):
            y_copy(i, d).wait_send()

    @pl.loop(0, nz - 1)
    def _(i):
        z_copy(i).wait_send()
        a_copy(i + 1).wait_send()

    @pl.loop(p + 1, np_)
    def _(q):
        @pl.loop(0, nz)
        def _(d):
            x_copy(q, d).wait_send()

    @pl.loop(1, group)
    def _(d):
        f_copy(d).wait_send()


def local(np_, nz, ny, right_side, prior_solution, factor_codes, block_scale, diag_inverse, inner_factor):
    rows, rhs = right_side.shape
    depth = prior_solution.shape[0]
    group = ny * 2
    row_block = rows * group
    half = rhs // 2
    chunk = half // ny
    width = diag_inverse.shape[-1]
    dma = pltpu.SemaphoreType.DMA
    scratch = [
        pltpu.VMEM((rows, rhs), F32),
        pltpu.VMEM((depth, rhs), BF16),
        pltpu.VMEM((nz, row_block, depth), BF16),
        pltpu.VMEM((rhs, depth), BF16),
        pltpu.VMEM((row_block, rhs), F32),
        pltpu.VMEM((2, half, row_block), F32),
        pltpu.VMEM((nz, half, row_block), BF16),
        pltpu.VMEM((nz, half, row_block), BF16),
        pltpu.VMEM((nz, ny, chunk, row_block), F32),
        pltpu.VMEM((nz, ny, chunk, row_block), BF16),
        pltpu.VMEM((nz, ny, chunk, row_block), BF16),
        pltpu.VMEM((nz, chunk, row_block), BF16),
        pltpu.VMEM((nz, chunk, row_block), BF16),
        pltpu.VMEM((np_, group, rows, width), BF16),
        pltpu.VMEM((nz, group, rows, row_block), BF16),
        pltpu.VMEM((row_block, row_block), F32),
        pltpu.VMEM((group, row_block, row_block), BF16),
        pltpu.VMEM((np_, nz, chunk, row_block), BF16),
        pltpu.VMEM((chunk, row_block), BF16),
        pltpu.VMEM((chunk, row_block), F32),
        pltpu.VMEM((group, rows, half), F32),
        pltpu.VMEM((group, rows, half), F32),
        dma((2,)),
        dma((nz,)),
        dma((np_,)),
        dma((np_, ny)),
        dma((np_, ny)),
        dma((np_, ny)),
        dma((np_, ny)),
        dma((group,)),
        dma((group,)),
        dma((2, nz // 2, 2)),
        dma((nz, 2)),
        dma((ny,)),
        dma((ny,)),
        dma((ny,)),
        dma((ny,)),
        dma((nz,)),
        dma((nz,)),
        dma((nz, ny)),
        dma((nz, ny)),
        dma((nz,)),
        dma((nz,)),
        dma((nz,)),
        dma((np_, nz)),
        dma((np_, nz)),
        dma((group,)),
        dma((group,)),
        pltpu.SemaphoreType.REGULAR((np_,)),
    ]
    anywhere = pl.BlockSpec(memory_space=pl.ANY)
    return pl.pallas_call(
        functools.partial(kernel, np_, nz, ny),
        out_shape=jax.ShapeDtypeStruct((rows, rhs), F32),
        in_specs=[anywhere, anywhere, anywhere, pl.BlockSpec(memory_space=pltpu.SMEM), anywhere, anywhere],
        out_specs=pl.BlockSpec(memory_space=pltpu.VMEM),
        scratch_shapes=scratch,
        compiler_params=pltpu.CompilerParams(collective_id=0, has_side_effects=True, vmem_limit_bytes=60 * 2**20),
        cost_estimate=pl.CostEstimate(
            flops=2 * nz * row_block * depth * rhs, bytes_accessed=2 * nz * row_block * depth, transcendentals=0
        ),
    )(right_side, prior_solution, factor_codes, block_scale, diag_inverse, inner_factor)


def build(mesh, ny):
    np_ = mesh.shape["row"]
    nz = mesh.shape["col"] // (2 * ny)
    return jax.shard_map(
        functools.partial(local, np_, nz, ny),
        mesh=mesh,
        in_specs=(
            P(("row", "col"), None),
            P("col", None),
            P("row", "col"),
            P("row", "col"),
            P("row", "col", None),
            P("row", None, "col", None),
        ),
        out_specs=P(("row", "col"), None),
        check_vma=False,
    )


def solution(mesh):
    return build(mesh, 4)
```

```python
import functools

import jax
import jax.numpy as jnp
from jax import lax
from jax.experimental import pallas as pl
from jax.experimental.pallas import tpu as pltpu
from jax.sharding import PartitionSpec as P

MESH = pl.DeviceIdType.MESH
F32, BF16 = jnp.float32, jnp.bfloat16


def dot_t(a, b):
    return lax.dot_general(a, b, (((1,), (1,)), ((), ())), preferred_element_type=F32)


def kernel(
    np_, nz, ny,
    right_ref, prior_ref, codes_ref, scale_ref, diag_ref, inner_ref, out_ref,
    right_v, scale_s, prior_v, codes_v, prior_t, place, pt, core_out, core_in, half_sum, y_out, y_in, z_out, z_in,
    w, lcol, macc, mw, act, x_out, res, final_out, final_in,
    in_sem, codes_sem, w_sem, wy_s, wy_r, wc_s, wc_r, la_s, la_r, l_s, l_r, my_s, my_r, mc_s, mc_r, c_s, c_r, y_s, y_r, z_s, z_r, a_s, a_r, x_s, f_s, f_r, ready,
):
    p, j = lax.axis_index("row"), lax.axis_index("col")
    group = ny * 2
    z, g = j // group, j % group
    y, c = g // 2, g % 2
    rows = right_ref.shape[0]
    blocks = scale_ref.shape[1]
    kb = prior_ref.shape[0] // blocks
    row_block = rows * group
    half = right_ref.shape[1] // 2
    chunk = half // ny
    last = jnp.maximum(p - 1, 0)
    y_near = sorted(range(1, ny), key=lambda d: min(d, ny - d))
    far_first = sorted(range(nz), key=lambda d: -min(d, nz - d))

    def col_of(z_, y_, c_):
        return z_ * group + y_ * 2 + c_

    def remote(src, dst, send, recv, row, col):
        return pltpu.make_async_remote_copy(
            src_ref=src, dst_ref=dst, send_sem=send, recv_sem=recv, device_id={"row": row, "col": col}, device_id_type=MESH
        )

    barrier = pltpu.get_barrier_semaphore()

    def greet(row, col):
        pl.semaphore_signal(barrier, inc=1, device_id={"row": row, "col": col}, device_id_type=MESH)

    greet(p, col_of(z, y, 1 - c))

    @pl.loop(1, ny)
    def _(d):
        greet(p, col_of(z, (y + d) % ny, c))
        greet(p, col_of(z, (y + d) % ny, 1 - c))

    @pl.loop(1, nz)
    def _(d):
        greet(p, col_of((z + d) % nz, y, c))

    @pl.loop(1, np_)
    def _(d):
        greet((p + d) % np_, j)

    load_prior = pltpu.make_async_copy(prior_ref, prior_v, in_sem.at[0])
    load_right = pltpu.make_async_copy(right_ref, right_v, in_sem.at[1])
    load_scale = pltpu.make_async_copy(scale_ref, scale_s, in_sem.at[2])
    load_scale.start()
    load_prior.start()
    load_right.start()

    def load_codes(i):
        zb = (z + 1 + i) % nz
        return pltpu.make_async_copy(
            codes_ref.at[pl.ds(pl.multiple_of(zb * row_block, row_block), row_block)], codes_v.at[i], codes_sem.at[i]
        )

    @pl.loop(0, nz)
    def _(i):
        load_codes(i).start()

    def load_inner(m):
        return pltpu.make_async_copy(inner_ref.at[0, m], w.at[m, g], w_sem.at[m])

    load_diag = pltpu.make_async_copy(diag_ref.at[0], w.at[p, g], w_sem.at[p])

    @pl.loop(0, p)
    def _(m):
        load_inner(m).start()

    load_diag.start()

    load_scale.wait()
    load_prior.wait()
    for b in range(blocks):
        part = prior_v[b * kb : (b + 1) * kb, :].astype(F32) * scale_s[0, b]
        prior_t[:, b * kb : (b + 1) * kb] = part.T.astype(BF16)
    load_right.wait()
    place[...] = jnp.zeros_like(place)
    place[pl.ds(pl.multiple_of(g * rows, rows), rows), :] = right_v[...]

    pl.semaphore_wait(barrier, 1 + 2 * (ny - 1) + (nz - 1) + (np_ - 1))

    @pl.loop(0, p)
    def _(q):
        pl.semaphore_signal(ready.at[p], inc=1, device_id={"row": q, "col": j}, device_id_type=MESH)

    def w_y(m, d):
        to = (y + d) % ny
        return remote(w.at[m, g], w.at[m, g], wy_s.at[m, d], wy_r.at[m, y], p, col_of(z, to, c))

    def w_y_arrival(m, d):
        src = (y + d) % ny
        slot = src * 2 + c
        return remote(w.at[m, slot], w.at[m, slot], wy_s.at[m, d], wy_r.at[m, src], p, col_of(z, src, c))

    def w_c(m, yy):
        slot = yy * 2 + c
        return remote(w.at[m, slot], w.at[m, slot], wc_s.at[m, yy], wc_r.at[m, yy], p, col_of(z, y, 1 - c))

    def w_c_arrival(m, yy):
        slot = yy * 2 + 1 - c
        return remote(w.at[m, slot], w.at[m, slot], wc_s.at[m, yy], wc_r.at[m, yy], p, col_of(z, y, 1 - c))

    load_diag.wait()

    @pl.loop(0, p)
    def _(m):
        load_inner(m).wait()

    def share(m):
        for d in y_near:
            w_y(m, d).start()

        w_c(m, y).start()

    def gathered(m):
        @pl.loop(0, ny)
        def _(yy):
            w_c_arrival(m, yy).wait_recv()

    def forward(m):
        for d in y_near:
            w_y_arrival(m, d).wait_recv()
            w_c(m, (y + d) % ny).start()

    own_columns = pl.ds(pl.multiple_of(g * row_block, row_block), row_block)

    def la_copy(d):
        to = (g + d) % group
        columns = pl.ds(pl.multiple_of(to * row_block, row_block), row_block)
        return remote(w.at[last, g, :, columns], lcol.at[z, g], la_s.at[d], la_r.at[g], p, z * group + to)

    def la_arrival(d):
        src = (g + d) % group
        return remote(lcol.at[z, src], lcol.at[z, src], la_s.at[d], la_r.at[src], p, z * group + src)

    far = nz // 2

    def l_half(owner, h):
        return lcol.at[owner, pl.ds(pl.multiple_of(h * (group // 2), group // 2), group // 2)]

    def l_move(k, h, way):
        step = 1 - 2 * way
        owner = (z + nz - (k - 1) * step) % nz
        to = (z + nz + step) % nz
        part = l_half(owner, h)
        return remote(part, part, l_s.at[way, k - 1, h], l_r.at[owner, h], p, col_of(to, y, c))

    def l_arrival(off, h):
        owner = (z + off) % nz
        part = l_half(owner, h)
        return remote(part, part, l_s.at[0, 0, h], l_r.at[owner, h], p, col_of((z + 1) % nz, y, c))

    def l_start(h):
        l_move(1, h, 0).start()
        if far > 1:
            l_move(1, h, 1).start()

    def l_pass(k, h):
        l_arrival(nz - k, h).wait_recv()
        l_move(k + 1, h, 0).start()

        @pl.when(k < far - 1)
        def _():
            l_arrival(k, h).wait_recv()
            l_move(k + 1, h, 1).start()

    @pl.when(p > 0)
    def _():
        @pl.loop(1, group)
        def _(d):
            la_copy(d).start()

        lcol[z, g] = w[last, g, :, own_columns]

    def m_y(d):
        to = (y + d) % ny
        return remote(mw.at[g], mw.at[g], my_s.at[d], my_r.at[y], p, col_of(z, to, c))

    def m_y_arrival(d):
        src = (y + d) % ny
        slot = src * 2 + c
        return remote(mw.at[slot], mw.at[slot], my_s.at[d], my_r.at[src], p, col_of(z, src, c))

    def m_c(yy):
        slot = yy * 2 + c
        return remote(mw.at[slot], mw.at[slot], mc_s.at[yy], mc_r.at[yy], p, col_of(z, y, 1 - c))

    def m_c_arrival(yy):
        slot = yy * 2 + 1 - c
        return remote(mw.at[slot], mw.at[slot], mc_s.at[yy], mc_r.at[yy], p, col_of(z, y, 1 - c))

    def core_copy(i):
        return remote(core_out.at[i], core_in.at[i], c_s.at[i], c_r.at[i], p, col_of(z, y, 1 - c))

    def y_copy(i, d):
        to = (y + d) % ny
        return remote(y_out.at[i, to], y_in.at[i, y], y_s.at[i, d], y_r.at[i, y], p, col_of(z, to, c))

    def y_arrival(i, d):
        src = (y + d) % ny
        return remote(y_out.at[i, src], y_in.at[i, src], y_s.at[i, d], y_r.at[i, src], p, col_of(z, src, c))

    def z_copy(i):
        to = (z + 1 + i) % nz
        return remote(z_out.at[i], z_in.at[z], z_s.at[i], z_r.at[z], p, col_of(to, y, c))

    def z_arrival(d):
        src = (z + d) % nz
        return remote(z_out.at[0], z_in.at[src], z_s.at[0], z_r.at[src], p, col_of(src, y, c))

    def across_y(i):
        core_copy(i).wait_recv()
        total = half_sum[i].reshape(half, row_block) + core_in[i].astype(F32)
        total = total.reshape(ny, chunk, row_block)
        half_sum[i] = total
        y_out[i] = total.astype(BF16)

        @pl.loop(1, ny)
        def _(d):
            y_copy(i, d).start()

    def across_z(i):
        total = half_sum[i, y]
        for d in range(1, ny):
            y_arrival(i, d).wait_recv()
            total = total + y_in[i, (y + d) % ny].astype(F32)
        return total

    lag = min(2, nz - 1)

    @pl.loop(0, nz)
    def _(i):
        load_codes(i).wait()
        pt[...] = dot_t(prior_t[...], codes_v[i]).reshape(2, half, row_block)

        @pl.when(i == nz - 1)
        def _():
            pt[...] -= place[...].T.reshape(2, half, row_block)

        core_out[i] = pt[1 - c].astype(BF16)
        core_copy(i).start()
        half_sum[i] = pt[c].reshape(ny, chunk, row_block)

        @pl.when(i >= lag)
        def _():
            across_y(i - lag)

        @pl.when((i == nz // 4) & (p > 0))
        def _():
            @pl.loop(1, group)
            def _(d):
                la_arrival(d).wait_recv()

            @pl.loop(0, 2)
            def _(h):
                l_start(h)

        if far > 1:

            @pl.when((i == nz - 1) & (p > 0))
            def _():
                @pl.loop(0, 2)
                def _(h):
                    l_pass(1, h)

    @pl.loop(nz - lag, nz)
    def _(i):
        across_y(i)

    share(p)

    def l_pass_both(k):
        if k < far:

            @pl.when(p > 0)
            def _():
                @pl.loop(0, 2)
                def _(h):
                    l_pass(k, h)

    @pl.loop(0, nz - 1)
    def _(i):
        z_out[i] = across_z(i).astype(BF16)
        z_copy(i).start()

        if far > 2:

            @pl.when((i == nz // 2) & (p > 0))
            def _():
                @pl.loop(0, 2)
                def _(h):
                    l_pass(2, h)

    @pl.loop(0, p - 1)
    def _(m):
        share(m)

    def a_copy(d):
        to = (z + d) % nz
        return remote(act.at[p, z], act.at[p, z], a_s.at[d], a_r.at[p, z], p, col_of(to, y, c))

    def send_current():
        act[p, z] = res[...].astype(BF16)

        for d in far_first[:-1]:
            a_copy(d).start()

    def act_arrival(s, src):
        return remote(x_out, act.at[s, src], x_s.at[0, 0], a_r.at[s, src], p, col_of(src, y, c))

    def times(s, own_here):
        total = jnp.zeros((chunk, row_block), F32)
        for d in far_first[::-1]:
            src = (z + d) % nz
            if not (own_here and d == 0):
                act_arrival(s, src).wait_recv()
            columns = pl.ds(pl.multiple_of(src * row_block, row_block), row_block)
            total = total + dot_t(act[s, src], w[s, :, :, columns].reshape(row_block, row_block))
        return total

    for k in range(3, far):
        l_pass_both(k)

    @pl.when(p > 0)
    def _():
        forward(p)
        gathered(p)

        def columns_of(d):
            return pl.ds(pl.multiple_of(((z + d) % nz) * row_block, row_block), row_block)

        def part(d, block):
            return jnp.dot(
                w[p, :, :, columns_of(d)].reshape(row_block, row_block),
                block.reshape(row_block, row_block),
                preferred_element_type=F32,
            )

        macc[...] = jnp.zeros_like(macc)

        @pl.loop(1, nz + 1)
        def _(t):
            off = (t + far) % nz

            @pl.when((off == far) | ((off == far - 1) & (off > 0)))
            def _():
                @pl.loop(0, 2)
                def _(h):
                    l_arrival(off, h).wait_recv()

            macc[...] += part(off, lcol[(z + off) % nz])

        mw[g] = macc[...].astype(BF16)

        for d in y_near:
            m_y(d).start()

        m_c(y).start()

    own = across_z(nz - 1)
    for d in range(1, nz):
        z_arrival(d).wait_recv()
        own = own + z_in[(z + d) % nz].astype(F32)
    res[...] = -own

    @pl.when(p <= 1)
    def _():
        send_current()

    @pl.when(p == 0)
    def _():
        forward(p)

    @pl.when(p > 0)
    def _():
        @pl.loop(0, p - 1)
        def _(m):
            forward(m)

        for d in y_near:
            m_y_arrival(d).wait_recv()
            m_c((y + d) % ny).start()

        @pl.loop(0, p - 1)
        def _(s):
            gathered(s)
            res[...] -= times(s, False)

    @pl.when(p > 1)
    def _():
        send_current()

    @pl.when(p == 0)
    def _():
        gathered(p)

    def shared(m):
        @pl.loop(1, ny)
        def _(d):
            w_y(m, d).wait_send()

        @pl.loop(0, ny)
        def _(yy):
            w_c(m, yy).wait_send()

    shared(p)

    @pl.loop(0, p - 1)
    def _(m):
        shared(m)

    @pl.when(p > 0)
    def _():
        @pl.loop(1, group)
        def _(d):
            la_copy(d).wait_send()

        @pl.loop(0, 2)
        def _(h):
            @pl.loop(1, far + 1)
            def _(k):
                l_move(k, h, 0).wait_send()

            @pl.loop(1, far)
            def _(k):
                l_move(k, h, 1).wait_send()

    @pl.loop(0, nz)
    def _(i):
        core_copy(i).wait_send()

        @pl.loop(1, ny)
        def _(d):
            y_copy(i, d).wait_send()

    @pl.loop(0, nz - 1)
    def _(i):
        z_copy(i).wait_send()

    res[...] = times(p, True)

    @pl.when(p > 0)
    def _():
        @pl.loop(0, ny)
        def _(yy):
            m_c_arrival(yy).wait_recv()

        total = jnp.zeros((chunk, row_block), F32)
        for d in far_first[::-1]:
            src = (z + d) % nz
            act_arrival(last, src).wait_recv()
            total = total + dot_t(act[last, src], mw[src])
        res[...] -= total

    solved = res[...]
    x_out[...] = solved.astype(BF16)

    def x_copy(q, d):
        to = (z + d) % nz
        return remote(x_out, act.at[p, z], x_s.at[q, d], a_r.at[p, z], q, col_of(to, y, c))

    @pl.loop(p + 1, np_)
    def _(q):
        pl.semaphore_wait(ready.at[q], 1)
        for d in far_first:
            x_copy(q, d).start()

    place[:half, :row_block] = jnp.zeros((half, row_block), F32)
    place[pl.ds(pl.multiple_of(y * chunk, chunk), chunk), :row_block] = solved
    final_out[...] = place[:half, :row_block].T.reshape(group, rows, half)

    def f_copy(d):
        to = (g + d) % group
        return remote(final_out.at[to], final_in.at[g], f_s.at[d], f_r.at[g], p, z * group + to)

    def f_arrival(d):
        src = (g + d) % group
        return remote(final_out.at[src], final_in.at[src], f_s.at[d], f_r.at[src], p, z * group + src)

    @pl.loop(1, group)
    def _(d):
        f_copy(d).start()

    final_in[g] = final_out[g]

    @pl.loop(1, group)
    def _(d):
        f_arrival(d).wait_recv()

    for cc in range(2):
        total = final_in[cc]
        for yy in range(1, ny):
            total = total + final_in[yy * 2 + cc]
        out_ref[:, cc * half : (cc + 1) * half] = total

    @pl.when(p > 0)
    def _():
        @pl.loop(1, ny)
        def _(d):
            m_y(d).wait_send()

        @pl.loop(0, ny)
        def _(yy):
            m_c(yy).wait_send()

    @pl.loop(1, nz)
    def _(d):
        a_copy(d).wait_send()

    @pl.loop(p + 1, np_)
    def _(q):
        @pl.loop(0, nz)
        def _(d):
            x_copy(q, d).wait_send()

    @pl.loop(1, group)
    def _(d):
        f_copy(d).wait_send()


def local(np_, nz, ny, right_side, prior_solution, factor_codes, block_scale, diag_inverse, inner_factor):
    rows, rhs = right_side.shape
    depth = prior_solution.shape[0]
    group = ny * 2
    row_block = rows * group
    half = rhs // 2
    chunk = half // ny
    width = diag_inverse.shape[-1]
    dma = pltpu.SemaphoreType.DMA
    scratch = [
        pltpu.VMEM((rows, rhs), F32),
        pltpu.SMEM(block_scale.shape, F32),
        pltpu.VMEM((depth, rhs), BF16),
        pltpu.VMEM((nz, row_block, depth), BF16),
        pltpu.VMEM((rhs, depth), BF16),
        pltpu.VMEM((row_block, rhs), F32),
        pltpu.VMEM((2, half, row_block), F32),
        pltpu.VMEM((nz, half, row_block), BF16),
        pltpu.VMEM((nz, half, row_block), BF16),
        pltpu.VMEM((nz, ny, chunk, row_block), F32),
        pltpu.VMEM((nz, ny, chunk, row_block), BF16),
        pltpu.VMEM((nz, ny, chunk, row_block), BF16),
        pltpu.VMEM((nz, chunk, row_block), BF16),
        pltpu.VMEM((nz, chunk, row_block), BF16),
        pltpu.VMEM((np_, group, rows, width), BF16),
        pltpu.VMEM((nz, group, rows, row_block), BF16),
        pltpu.VMEM((row_block, row_block), F32),
        pltpu.VMEM((group, row_block, row_block), BF16),
        pltpu.VMEM((np_, nz, chunk, row_block), BF16),
        pltpu.VMEM((chunk, row_block), BF16),
        pltpu.VMEM((chunk, row_block), F32),
        pltpu.VMEM((group, rows, half), F32),
        pltpu.VMEM((group, rows, half), F32),
        dma((3,)),
        dma((nz,)),
        dma((np_,)),
        dma((np_, ny)),
        dma((np_, ny)),
        dma((np_, ny)),
        dma((np_, ny)),
        dma((group,)),
        dma((group,)),
        dma((2, nz // 2, 2)),
        dma((nz, 2)),
        dma((ny,)),
        dma((ny,)),
        dma((ny,)),
        dma((ny,)),
        dma((nz,)),
        dma((nz,)),
        dma((nz, ny)),
        dma((nz, ny)),
        dma((nz,)),
        dma((nz,)),
        dma((nz,)),
        dma((np_, nz)),
        dma((np_, nz)),
        dma((group,)),
        dma((group,)),
        pltpu.SemaphoreType.REGULAR((np_,)),
    ]
    anywhere = pl.BlockSpec(memory_space=pl.ANY)
    return pl.pallas_call(
        functools.partial(kernel, np_, nz, ny),
        out_shape=jax.ShapeDtypeStruct((rows, rhs), F32),
        in_specs=[anywhere] * 6,
        out_specs=pl.BlockSpec(memory_space=pltpu.VMEM),
        scratch_shapes=scratch,
        compiler_params=pltpu.CompilerParams(collective_id=0, has_side_effects=True, vmem_limit_bytes=54 * 2**20 - 2**17),
        cost_estimate=pl.CostEstimate(
            flops=2 * nz * row_block * depth * rhs, bytes_accessed=2 * nz * row_block * depth, transcendentals=0
        ),
    )(right_side, prior_solution, factor_codes, block_scale, diag_inverse, inner_factor)


def build(mesh, ny):
    np_ = mesh.shape["row"]
    nz = mesh.shape["col"] // (2 * ny)
    return jax.shard_map(
        functools.partial(local, np_, nz, ny),
        mesh=mesh,
        in_specs=(
            P(("row", "col"), None),
            P("col", None),
            P("row", "col"),
            P("row", "col"),
            P("row", "col", None),
            P("row", None, "col", None),
        ),
        out_specs=P(("row", "col"), None),
        check_vma=False,
    )


def solution(mesh):
    return build(mesh, 4)
```

```python
import functools

import jax
import jax.numpy as jnp
from jax import lax
from jax.experimental import pallas as pl
from jax.experimental.pallas import tpu as pltpu
from jax.sharding import PartitionSpec as P

MESH = pl.DeviceIdType.MESH
F32, BF16 = jnp.float32, jnp.bfloat16


def dot_t(a, b):
    return lax.dot_general(a, b, (((1,), (1,)), ((), ())), preferred_element_type=F32)


def kernel(
    np_, nz, ny,
    right_ref, prior_ref, codes_ref, scale_ref, diag_ref, inner_ref, out_ref,
    right_v, scale_s, prior_v, codes_v, prior_t, place, pt, core_out, core_in, half_sum, y_out, y_in, z_out, z_in,
    w, lcol, macc, mw, act, x_out, res, final_out, final_in,
    in_sem, codes_sem, w_sem, wy_s, wy_r, wc_s, wc_r, la_s, la_r, l_s, l_r, my_s, my_r, mc_s, mc_r, c_s, c_r, y_s, y_r, z_s, z_r, a_s, a_r, x_s, f_s, f_r, ready,
):
    p, j = lax.axis_index("row"), lax.axis_index("col")
    group = ny * 2
    z, g = j // group, j % group
    y, c = g // 2, g % 2
    rows = right_ref.shape[0]
    blocks = scale_ref.shape[1]
    kb = prior_ref.shape[0] // blocks
    row_block = rows * group
    half = right_ref.shape[1] // 2
    chunk = half // ny
    last = jnp.maximum(p - 1, 0)
    y_near = sorted(range(1, ny), key=lambda d: min(d, ny - d))
    far_first = sorted(range(nz), key=lambda d: -min(d, nz - d))

    def col_of(z_, y_, c_):
        return z_ * group + y_ * 2 + c_

    def remote(src, dst, send, recv, row, col):
        return pltpu.make_async_remote_copy(
            src_ref=src, dst_ref=dst, send_sem=send, recv_sem=recv, device_id={"row": row, "col": col}, device_id_type=MESH
        )

    barrier = pltpu.get_barrier_semaphore()

    def greet(row, col):
        pl.semaphore_signal(barrier, inc=1, device_id={"row": row, "col": col}, device_id_type=MESH)

    greet(p, col_of(z, y, 1 - c))

    @pl.loop(1, ny)
    def _(d):
        greet(p, col_of(z, (y + d) % ny, c))
        greet(p, col_of(z, (y + d) % ny, 1 - c))

    @pl.loop(1, nz)
    def _(d):
        greet(p, col_of((z + d) % nz, y, c))

    @pl.loop(1, np_)
    def _(d):
        greet((p + d) % np_, j)

    load_prior = pltpu.make_async_copy(prior_ref, prior_v, in_sem.at[0])
    load_right = pltpu.make_async_copy(right_ref, right_v, in_sem.at[1])
    load_scale = pltpu.make_async_copy(scale_ref, scale_s, in_sem.at[2])
    load_scale.start()
    load_prior.start()
    load_right.start()

    def load_codes(i):
        zb = (z + 1 + i) % nz
        return pltpu.make_async_copy(
            codes_ref.at[pl.ds(pl.multiple_of(zb * row_block, row_block), row_block)], codes_v.at[i], codes_sem.at[i]
        )

    @pl.loop(0, nz)
    def _(i):
        load_codes(i).start()

    def load_inner(m):
        return pltpu.make_async_copy(inner_ref.at[0, m], w.at[m, g], w_sem.at[m])

    load_diag = pltpu.make_async_copy(diag_ref.at[0], w.at[p, g], w_sem.at[p])

    @pl.loop(0, p)
    def _(m):
        load_inner(m).start()

    load_diag.start()

    load_scale.wait()
    load_prior.wait()
    for b in range(blocks):
        part = prior_v[b * kb : (b + 1) * kb, :].astype(F32) * scale_s[0, b]
        prior_t[:, b * kb : (b + 1) * kb] = part.T.astype(BF16)
    load_right.wait()
    place[...] = jnp.zeros_like(place)
    place[pl.ds(pl.multiple_of(g * rows, rows), rows), :] = right_v[...]

    pl.semaphore_wait(barrier, 1 + 2 * (ny - 1) + (nz - 1) + (np_ - 1))

    @pl.loop(0, p)
    def _(q):
        pl.semaphore_signal(ready.at[p], inc=1, device_id={"row": q, "col": j}, device_id_type=MESH)

    def w_y(m, d):
        to = (y + d) % ny
        return remote(w.at[m, g], w.at[m, g], wy_s.at[m, d], wy_r.at[m, y], p, col_of(z, to, c))

    def w_y_arrival(m, d):
        src = (y + d) % ny
        slot = src * 2 + c
        return remote(w.at[m, slot], w.at[m, slot], wy_s.at[m, d], wy_r.at[m, src], p, col_of(z, src, c))

    def w_c(m, yy):
        slot = yy * 2 + c
        return remote(w.at[m, slot], w.at[m, slot], wc_s.at[m, yy], wc_r.at[m, yy], p, col_of(z, y, 1 - c))

    def w_c_arrival(m, yy):
        slot = yy * 2 + 1 - c
        return remote(w.at[m, slot], w.at[m, slot], wc_s.at[m, yy], wc_r.at[m, yy], p, col_of(z, y, 1 - c))

    load_diag.wait()

    @pl.loop(0, p)
    def _(m):
        load_inner(m).wait()

    def share(m):
        for d in y_near:
            w_y(m, d).start()

        w_c(m, y).start()

    def gathered(m):
        @pl.loop(0, ny)
        def _(yy):
            w_c_arrival(m, yy).wait_recv()

    def forward(m):
        for d in y_near:
            w_y_arrival(m, d).wait_recv()
            w_c(m, (y + d) % ny).start()

    own_columns = pl.ds(pl.multiple_of(g * row_block, row_block), row_block)

    def la_copy(d):
        to = (g + d) % group
        columns = pl.ds(pl.multiple_of(to * row_block, row_block), row_block)
        return remote(w.at[last, g, :, columns], lcol.at[z, g], la_s.at[d], la_r.at[g], p, z * group + to)

    def la_arrival(d):
        src = (g + d) % group
        return remote(lcol.at[z, src], lcol.at[z, src], la_s.at[d], la_r.at[src], p, z * group + src)

    far = nz // 2

    def l_half(owner, h):
        return lcol.at[owner, pl.ds(pl.multiple_of(h * (group // 2), group // 2), group // 2)]

    def l_move(k, h, way):
        step = 1 - 2 * way
        owner = (z + nz - (k - 1) * step) % nz
        to = (z + nz + step) % nz
        part = l_half(owner, h)
        return remote(part, part, l_s.at[way, k - 1, h], l_r.at[owner, h], p, col_of(to, y, c))

    def l_arrival(off, h):
        owner = (z + off) % nz
        part = l_half(owner, h)
        return remote(part, part, l_s.at[0, 0, h], l_r.at[owner, h], p, col_of((z + 1) % nz, y, c))

    def l_start(h):
        l_move(1, h, 0).start()
        if far > 1:
            l_move(1, h, 1).start()

    def l_pass(k, h):
        l_arrival(nz - k, h).wait_recv()
        l_move(k + 1, h, 0).start()

        @pl.when(k < far - 1)
        def _():
            l_arrival(k, h).wait_recv()
            l_move(k + 1, h, 1).start()

    @pl.when(p > 0)
    def _():
        @pl.loop(1, group)
        def _(d):
            la_copy(d).start()

        lcol[z, g] = w[last, g, :, own_columns]

    def m_y(d):
        to = (y + d) % ny
        return remote(mw.at[g], mw.at[g], my_s.at[d], my_r.at[y], p, col_of(z, to, c))

    def m_y_arrival(d):
        src = (y + d) % ny
        slot = src * 2 + c
        return remote(mw.at[slot], mw.at[slot], my_s.at[d], my_r.at[src], p, col_of(z, src, c))

    def m_c(yy):
        slot = yy * 2 + c
        return remote(mw.at[slot], mw.at[slot], mc_s.at[yy], mc_r.at[yy], p, col_of(z, y, 1 - c))

    def m_c_arrival(yy):
        slot = yy * 2 + 1 - c
        return remote(mw.at[slot], mw.at[slot], mc_s.at[yy], mc_r.at[yy], p, col_of(z, y, 1 - c))

    def core_copy(i):
        return remote(core_out.at[i], core_in.at[i], c_s.at[i], c_r.at[i], p, col_of(z, y, 1 - c))

    def y_copy(i, d):
        to = (y + d) % ny
        return remote(y_out.at[i, to], y_in.at[i, y], y_s.at[i, d], y_r.at[i, y], p, col_of(z, to, c))

    def y_arrival(i, d):
        src = (y + d) % ny
        return remote(y_out.at[i, src], y_in.at[i, src], y_s.at[i, d], y_r.at[i, src], p, col_of(z, src, c))

    def z_copy(i):
        to = (z + 1 + i) % nz
        return remote(z_out.at[i], z_in.at[z], z_s.at[i], z_r.at[z], p, col_of(to, y, c))

    def z_arrival(d):
        src = (z + d) % nz
        return remote(z_out.at[0], z_in.at[src], z_s.at[0], z_r.at[src], p, col_of(src, y, c))

    def across_y(i):
        core_copy(i).wait_recv()
        total = half_sum[i].reshape(half, row_block) + core_in[i].astype(F32)
        total = total.reshape(ny, chunk, row_block)
        half_sum[i] = total
        y_out[i] = total.astype(BF16)

        @pl.loop(1, ny)
        def _(d):
            y_copy(i, d).start()

    def across_z(i):
        total = half_sum[i, y]
        for d in range(1, ny):
            y_arrival(i, d).wait_recv()
            total = total + y_in[i, (y + d) % ny].astype(F32)
        return total

    lag = min(2, nz - 1)

    @pl.loop(0, nz)
    def _(i):
        load_codes(i).wait()
        pt[...] = dot_t(prior_t[...], codes_v[i]).reshape(2, half, row_block)

        @pl.when(i == nz - 1)
        def _():
            pt[...] -= place[...].T.reshape(2, half, row_block)

        core_out[i] = pt[1 - c].astype(BF16)
        core_copy(i).start()
        half_sum[i] = pt[c].reshape(ny, chunk, row_block)

        @pl.when(i >= lag)
        def _():
            across_y(i - lag)

        @pl.when((i == nz // 4) & (p > 0))
        def _():
            @pl.loop(1, group)
            def _(d):
                la_arrival(d).wait_recv()

            @pl.loop(0, 2)
            def _(h):
                l_start(h)

        if far > 1:

            @pl.when((i == nz - 1) & (p > 0))
            def _():
                @pl.loop(0, 2)
                def _(h):
                    l_pass(1, h)

    @pl.loop(nz - lag, nz)
    def _(i):
        across_y(i)

    share(p)

    def l_pass_both(k):
        if k < far:

            @pl.when(p > 0)
            def _():
                @pl.loop(0, 2)
                def _(h):
                    l_pass(k, h)

    @pl.loop(0, nz - 1)
    def _(i):
        z_out[i] = across_z(i).astype(BF16)
        z_copy(i).start()

        if far > 2:

            @pl.when((i == nz // 2) & (p > 0))
            def _():
                @pl.loop(0, 2)
                def _(h):
                    l_pass(2, h)

    @pl.loop(0, p - 1)
    def _(m):
        share(m)

    def a_copy(d):
        to = (z + d) % nz
        return remote(act.at[p, z], act.at[p, z], a_s.at[d], a_r.at[p, z], p, col_of(to, y, c))

    def send_current():
        act[p, z] = res[...].astype(BF16)

        for d in far_first[:-1]:
            a_copy(d).start()

    def act_arrival(s, src):
        return remote(x_out, act.at[s, src], x_s.at[0, 0], a_r.at[s, src], p, col_of(src, y, c))

    def times(s, own_here):
        total = jnp.zeros((chunk, row_block), F32)
        for d in far_first[::-1]:
            src = (z + d) % nz
            if not (own_here and d == 0):
                act_arrival(s, src).wait_recv()
            columns = pl.ds(pl.multiple_of(src * row_block, row_block), row_block)
            total = total + dot_t(act[s, src], w[s, :, :, columns].reshape(row_block, row_block))
        return total

    for k in range(3, far):
        l_pass_both(k)

    @pl.when(p > 0)
    def _():
        forward(p)
        gathered(p)

        def columns_of(d):
            return pl.ds(pl.multiple_of(((z + d) % nz) * row_block, row_block), row_block)

        def part(d, block):
            return jnp.dot(
                w[p, :, :, columns_of(d)].reshape(row_block, row_block),
                block.reshape(row_block, row_block),
                preferred_element_type=F32,
            )

        macc[...] = jnp.zeros_like(macc)

        @pl.loop(1, nz + 1)
        def _(t):
            off = (t + far) % nz

            @pl.when((off == far) | ((off == far - 1) & (off > 0)))
            def _():
                @pl.loop(0, 2)
                def _(h):
                    l_arrival(off, h).wait_recv()

            macc[...] += part(off, lcol[(z + off) % nz])

        mw[g] = macc[...].astype(BF16)

        for d in y_near:
            m_y(d).start()

        m_c(y).start()

    own = across_z(nz - 1)
    for d in range(1, nz):
        z_arrival(d).wait_recv()
        own = own + z_in[(z + d) % nz].astype(F32)
    res[...] = -own

    @pl.when(p <= 1)
    def _():
        send_current()

    @pl.when(p == 0)
    def _():
        forward(p)

    @pl.when(p > 0)
    def _():
        @pl.loop(0, p - 1)
        def _(m):
            forward(m)

        for d in y_near:
            m_y_arrival(d).wait_recv()
            m_c((y + d) % ny).start()

        @pl.loop(0, p - 1)
        def _(s):
            gathered(s)
            res[...] -= times(s, False)

    @pl.when(p > 1)
    def _():
        send_current()

    @pl.when(p == 0)
    def _():
        gathered(p)

    def shared(m):
        @pl.loop(1, ny)
        def _(d):
            w_y(m, d).wait_send()

        @pl.loop(0, ny)
        def _(yy):
            w_c(m, yy).wait_send()

    shared(p)

    @pl.loop(0, p - 1)
    def _(m):
        shared(m)

    @pl.when(p > 0)
    def _():
        @pl.loop(1, group)
        def _(d):
            la_copy(d).wait_send()

        @pl.loop(0, 2)
        def _(h):
            @pl.loop(1, far + 1)
            def _(k):
                l_move(k, h, 0).wait_send()

            @pl.loop(1, far)
            def _(k):
                l_move(k, h, 1).wait_send()

    @pl.loop(0, nz)
    def _(i):
        core_copy(i).wait_send()

        @pl.loop(1, ny)
        def _(d):
            y_copy(i, d).wait_send()

    @pl.loop(0, nz - 1)
    def _(i):
        z_copy(i).wait_send()

    res[...] = times(p, True)

    @pl.when(p > 0)
    def _():
        @pl.loop(0, ny)
        def _(yy):
            m_c_arrival(yy).wait_recv()

        total = jnp.zeros((chunk, row_block), F32)
        for d in far_first[::-1]:
            src = (z + d) % nz
            act_arrival(last, src).wait_recv()
            total = total + dot_t(act[last, src], mw[src])
        res[...] -= total

    solved = res[...]
    x_out[...] = solved.astype(BF16)

    def x_copy(q, d):
        to = (z + d) % nz
        return remote(x_out, act.at[p, z], x_s.at[q, d], a_r.at[p, z], q, col_of(to, y, c))

    @pl.loop(0, np_ - 1 - p)
    def _(i):
        q = np_ - 1 - i
        pl.semaphore_wait(ready.at[q], 1)
        for d in far_first:
            x_copy(q, d).start()

    place[:half, :row_block] = jnp.zeros((half, row_block), F32)
    place[pl.ds(pl.multiple_of(y * chunk, chunk), chunk), :row_block] = solved
    final_out[...] = place[:half, :row_block].T.reshape(group, rows, half)

    def f_copy(d):
        to = (g + d) % group
        return remote(final_out.at[to], final_in.at[g], f_s.at[d], f_r.at[g], p, z * group + to)

    def f_arrival(d):
        src = (g + d) % group
        return remote(final_out.at[src], final_in.at[src], f_s.at[d], f_r.at[src], p, z * group + src)

    @pl.loop(1, group)
    def _(d):
        f_copy(d).start()

    final_in[g] = final_out[g]

    @pl.loop(1, group)
    def _(d):
        f_arrival(d).wait_recv()

    for cc in range(2):
        total = final_in[cc]
        for yy in range(1, ny):
            total = total + final_in[yy * 2 + cc]
        out_ref[:, cc * half : (cc + 1) * half] = total

    @pl.when(p > 0)
    def _():
        @pl.loop(1, ny)
        def _(d):
            m_y(d).wait_send()

        @pl.loop(0, ny)
        def _(yy):
            m_c(yy).wait_send()

    @pl.loop(1, nz)
    def _(d):
        a_copy(d).wait_send()

    @pl.loop(p + 1, np_)
    def _(q):
        @pl.loop(0, nz)
        def _(d):
            x_copy(q, d).wait_send()

    @pl.loop(1, group)
    def _(d):
        f_copy(d).wait_send()


def local(np_, nz, ny, right_side, prior_solution, factor_codes, block_scale, diag_inverse, inner_factor):
    rows, rhs = right_side.shape
    depth = prior_solution.shape[0]
    group = ny * 2
    row_block = rows * group
    half = rhs // 2
    chunk = half // ny
    width = diag_inverse.shape[-1]
    dma = pltpu.SemaphoreType.DMA
    scratch = [
        pltpu.VMEM((rows, rhs), F32),
        pltpu.SMEM(block_scale.shape, F32),
        pltpu.VMEM((depth, rhs), BF16),
        pltpu.VMEM((nz, row_block, depth), BF16),
        pltpu.VMEM((rhs, depth), BF16),
        pltpu.VMEM((row_block, rhs), F32),
        pltpu.VMEM((2, half, row_block), F32),
        pltpu.VMEM((nz, half, row_block), BF16),
        pltpu.VMEM((nz, half, row_block), BF16),
        pltpu.VMEM((nz, ny, chunk, row_block), F32),
        pltpu.VMEM((nz, ny, chunk, row_block), BF16),
        pltpu.VMEM((nz, ny, chunk, row_block), BF16),
        pltpu.VMEM((nz, chunk, row_block), BF16),
        pltpu.VMEM((nz, chunk, row_block), BF16),
        pltpu.VMEM((np_, group, rows, width), BF16),
        pltpu.VMEM((nz, group, rows, row_block), BF16),
        pltpu.VMEM((row_block, row_block), F32),
        pltpu.VMEM((group, row_block, row_block), BF16),
        pltpu.VMEM((np_, nz, chunk, row_block), BF16),
        pltpu.VMEM((chunk, row_block), BF16),
        pltpu.VMEM((chunk, row_block), F32),
        pltpu.VMEM((group, rows, half), F32),
        pltpu.VMEM((group, rows, half), F32),
        dma((3,)),
        dma((nz,)),
        dma((np_,)),
        dma((np_, ny)),
        dma((np_, ny)),
        dma((np_, ny)),
        dma((np_, ny)),
        dma((group,)),
        dma((group,)),
        dma((2, nz // 2, 2)),
        dma((nz, 2)),
        dma((ny,)),
        dma((ny,)),
        dma((ny,)),
        dma((ny,)),
        dma((nz,)),
        dma((nz,)),
        dma((nz, ny)),
        dma((nz, ny)),
        dma((nz,)),
        dma((nz,)),
        dma((nz,)),
        dma((np_, nz)),
        dma((np_, nz)),
        dma((group,)),
        dma((group,)),
        pltpu.SemaphoreType.REGULAR((np_,)),
    ]
    anywhere = pl.BlockSpec(memory_space=pl.ANY)
    return pl.pallas_call(
        functools.partial(kernel, np_, nz, ny),
        out_shape=jax.ShapeDtypeStruct((rows, rhs), F32),
        in_specs=[anywhere] * 6,
        out_specs=pl.BlockSpec(memory_space=pltpu.VMEM),
        scratch_shapes=scratch,
        compiler_params=pltpu.CompilerParams(collective_id=0, has_side_effects=True, vmem_limit_bytes=54 * 2**20 - 2**17),
        cost_estimate=pl.CostEstimate(
            flops=2 * nz * row_block * depth * rhs, bytes_accessed=2 * nz * row_block * depth, transcendentals=0
        ),
    )(right_side, prior_solution, factor_codes, block_scale, diag_inverse, inner_factor)


def build(mesh, ny):
    np_ = mesh.shape["row"]
    nz = mesh.shape["col"] // (2 * ny)
    return jax.shard_map(
        functools.partial(local, np_, nz, ny),
        mesh=mesh,
        in_specs=(
            P(("row", "col"), None),
            P("col", None),
            P("row", "col"),
            P("row", "col"),
            P("row", "col", None),
            P("row", None, "col", None),
        ),
        out_specs=P(("row", "col"), None),
        check_vma=False,
    )


def solution(mesh):
    return build(mesh, 4)
```

```python
import functools

import jax
import jax.numpy as jnp
from jax import lax
from jax.experimental import pallas as pl
from jax.experimental.pallas import tpu as pltpu
from jax.sharding import PartitionSpec as P

MESH = pl.DeviceIdType.MESH
F32, BF16 = jnp.float32, jnp.bfloat16


def dot_t(a, b):
    return lax.dot_general(a, b, (((1,), (1,)), ((), ())), preferred_element_type=F32)


def kernel(
    np_, nz, ny,
    right_ref, prior_ref, codes_ref, scale_ref, diag_ref, inner_ref, out_ref,
    right_v, scale_s, prior_v, codes_v, prior_t, place, pt, core_out, core_in, half_sum, y_out, y_in, z_out, z_in,
    w, lcol, macc, mw, act, x_out, res, final_out, final_in,
    in_sem, codes_sem, w_sem, wy_s, wy_r, wc_s, wc_r, la_s, la_r, l_s, l_r, my_s, my_r, mc_s, mc_r, c_s, c_r, y_s, y_r, z_s, z_r, a_s, a_r, x_s, f_s, f_r, ready,
):
    p, j = lax.axis_index("row"), lax.axis_index("col")
    group = ny * 2
    z, g = j // group, j % group
    y, c = g // 2, g % 2
    rows = right_ref.shape[0]
    blocks = scale_ref.shape[1]
    kb = prior_ref.shape[0] // blocks
    row_block = rows * group
    half = right_ref.shape[1] // 2
    chunk = half // ny
    last = jnp.maximum(p - 1, 0)
    y_near = sorted(range(1, ny), key=lambda d: min(d, ny - d))
    far_first = sorted(range(nz), key=lambda d: -min(d, nz - d))

    def col_of(z_, y_, c_):
        return z_ * group + y_ * 2 + c_

    def remote(src, dst, send, recv, row, col):
        return pltpu.make_async_remote_copy(
            src_ref=src, dst_ref=dst, send_sem=send, recv_sem=recv, device_id={"row": row, "col": col}, device_id_type=MESH
        )

    barrier = pltpu.get_barrier_semaphore()

    def greet(row, col):
        pl.semaphore_signal(barrier, inc=1, device_id={"row": row, "col": col}, device_id_type=MESH)

    greet(p, col_of(z, y, 1 - c))

    @pl.loop(1, ny)
    def _(d):
        greet(p, col_of(z, (y + d) % ny, c))
        greet(p, col_of(z, (y + d) % ny, 1 - c))

    @pl.loop(1, nz)
    def _(d):
        greet(p, col_of((z + d) % nz, y, c))

    @pl.loop(1, np_)
    def _(d):
        greet((p + d) % np_, j)

    load_prior = pltpu.make_async_copy(prior_ref, prior_v, in_sem.at[0])
    load_right = pltpu.make_async_copy(right_ref, right_v, in_sem.at[1])
    load_scale = pltpu.make_async_copy(scale_ref, scale_s, in_sem.at[2])
    load_scale.start()
    load_prior.start()
    load_right.start()

    def load_codes(i):
        zb = (z + 1 + i) % nz
        return pltpu.make_async_copy(
            codes_ref.at[pl.ds(pl.multiple_of(zb * row_block, row_block), row_block)], codes_v.at[i], codes_sem.at[i]
        )

    @pl.loop(0, nz)
    def _(i):
        load_codes(i).start()

    def load_inner(m):
        return pltpu.make_async_copy(inner_ref.at[0, m], w.at[m, g], w_sem.at[m])

    load_diag = pltpu.make_async_copy(diag_ref.at[0], w.at[p, g], w_sem.at[p])

    @pl.loop(0, p)
    def _(m):
        load_inner(m).start()

    load_diag.start()

    load_scale.wait()
    load_prior.wait()
    for b in range(blocks):
        part = prior_v[b * kb : (b + 1) * kb, :].astype(F32) * scale_s[0, b]
        prior_t[:, b * kb : (b + 1) * kb] = part.T.astype(BF16)
    load_right.wait()
    place[...] = jnp.zeros_like(place)
    place[pl.ds(pl.multiple_of(g * rows, rows), rows), :] = right_v[...]

    pl.semaphore_wait(barrier, 1 + 2 * (ny - 1) + (nz - 1) + (np_ - 1))

    @pl.loop(0, p)
    def _(q):
        pl.semaphore_signal(ready.at[p], inc=1, device_id={"row": q, "col": j}, device_id_type=MESH)

    def w_y(m, d):
        to = (y + d) % ny
        return remote(w.at[m, g], w.at[m, g], wy_s.at[m, d], wy_r.at[m, y], p, col_of(z, to, c))

    def w_y_arrival(m, d):
        src = (y + d) % ny
        slot = src * 2 + c
        return remote(w.at[m, slot], w.at[m, slot], wy_s.at[m, d], wy_r.at[m, src], p, col_of(z, src, c))

    def w_c(m, yy):
        slot = yy * 2 + c
        return remote(w.at[m, slot], w.at[m, slot], wc_s.at[m, yy], wc_r.at[m, yy], p, col_of(z, y, 1 - c))

    def w_c_arrival(m, yy):
        slot = yy * 2 + 1 - c
        return remote(w.at[m, slot], w.at[m, slot], wc_s.at[m, yy], wc_r.at[m, yy], p, col_of(z, y, 1 - c))

    load_diag.wait()

    @pl.loop(0, p)
    def _(m):
        load_inner(m).wait()

    def share(m):
        for d in y_near:
            w_y(m, d).start()

        w_c(m, y).start()

    def gathered(m):
        @pl.loop(0, ny)
        def _(yy):
            w_c_arrival(m, yy).wait_recv()

    def forward(m):
        for d in y_near:
            w_y_arrival(m, d).wait_recv()
            w_c(m, (y + d) % ny).start()

    own_columns = pl.ds(pl.multiple_of(g * row_block, row_block), row_block)

    def la_copy(d):
        to = (g + d) % group
        columns = pl.ds(pl.multiple_of(to * row_block, row_block), row_block)
        return remote(w.at[last, g, :, columns], lcol.at[z, g], la_s.at[d], la_r.at[g], p, z * group + to)

    def la_arrival(d):
        src = (g + d) % group
        return remote(lcol.at[z, src], lcol.at[z, src], la_s.at[d], la_r.at[src], p, z * group + src)

    far = nz // 2

    def l_half(owner, h):
        return lcol.at[owner, pl.ds(pl.multiple_of(h * (group // 2), group // 2), group // 2)]

    def l_move(k, h, way):
        step = 1 - 2 * way
        owner = (z + nz - (k - 1) * step) % nz
        to = (z + nz + step) % nz
        part = l_half(owner, h)
        return remote(part, part, l_s.at[way, k - 1, h], l_r.at[owner, h], p, col_of(to, y, c))

    def l_arrival(off, h):
        owner = (z + off) % nz
        part = l_half(owner, h)
        return remote(part, part, l_s.at[0, 0, h], l_r.at[owner, h], p, col_of((z + 1) % nz, y, c))

    def l_start(h):
        l_move(1, h, 0).start()
        if far > 1:
            l_move(1, h, 1).start()

    def l_pass(k, h):
        l_arrival(nz - k, h).wait_recv()
        l_move(k + 1, h, 0).start()

        @pl.when(k < far - 1)
        def _():
            l_arrival(k, h).wait_recv()
            l_move(k + 1, h, 1).start()

    @pl.when(p > 0)
    def _():
        @pl.loop(1, group)
        def _(d):
            la_copy(d).start()

        lcol[z, g] = w[last, g, :, own_columns]

    def m_y(d):
        to = (y + d) % ny
        return remote(mw.at[g], mw.at[g], my_s.at[d], my_r.at[y], p, col_of(z, to, c))

    def m_y_arrival(d):
        src = (y + d) % ny
        slot = src * 2 + c
        return remote(mw.at[slot], mw.at[slot], my_s.at[d], my_r.at[src], p, col_of(z, src, c))

    def m_c(yy):
        slot = yy * 2 + c
        return remote(mw.at[slot], mw.at[slot], mc_s.at[yy], mc_r.at[yy], p, col_of(z, y, 1 - c))

    def m_c_arrival(yy):
        slot = yy * 2 + 1 - c
        return remote(mw.at[slot], mw.at[slot], mc_s.at[yy], mc_r.at[yy], p, col_of(z, y, 1 - c))

    def core_copy(i):
        return remote(core_out.at[i], core_in.at[i], c_s.at[i], c_r.at[i], p, col_of(z, y, 1 - c))

    def y_copy(i, d):
        to = (y + d) % ny
        return remote(y_out.at[i, to], y_in.at[i, y], y_s.at[i, d], y_r.at[i, y], p, col_of(z, to, c))

    def y_arrival(i, d):
        src = (y + d) % ny
        return remote(y_out.at[i, src], y_in.at[i, src], y_s.at[i, d], y_r.at[i, src], p, col_of(z, src, c))

    def z_copy(i):
        to = (z + 1 + i) % nz
        return remote(z_out.at[i], z_in.at[z], z_s.at[i], z_r.at[z], p, col_of(to, y, c))

    def z_arrival(d):
        src = (z + d) % nz
        return remote(z_out.at[0], z_in.at[src], z_s.at[0], z_r.at[src], p, col_of(src, y, c))

    def across_y(i):
        core_copy(i).wait_recv()
        total = half_sum[i].reshape(half, row_block) + core_in[i].astype(F32)
        total = total.reshape(ny, chunk, row_block)
        half_sum[i] = total
        y_out[i] = total.astype(BF16)

        @pl.loop(1, ny)
        def _(d):
            y_copy(i, d).start()

    def across_z(i):
        total = half_sum[i, y]
        for d in range(1, ny):
            y_arrival(i, d).wait_recv()
            total = total + y_in[i, (y + d) % ny].astype(F32)
        return total

    lag = min(2, nz - 1)

    @pl.loop(0, nz)
    def _(i):
        load_codes(i).wait()
        pt[...] = dot_t(prior_t[...], codes_v[i]).reshape(2, half, row_block)

        @pl.when(i == nz - 1)
        def _():
            pt[...] -= place[...].T.reshape(2, half, row_block)

        core_out[i] = pt[1 - c].astype(BF16)
        core_copy(i).start()
        half_sum[i] = pt[c].reshape(ny, chunk, row_block)

        @pl.when(i >= lag)
        def _():
            across_y(i - lag)

        @pl.when((i == nz // 4) & (p > 0))
        def _():
            @pl.loop(1, group)
            def _(d):
                la_arrival(d).wait_recv()

            @pl.loop(0, 2)
            def _(h):
                l_start(h)

        if far > 1:

            @pl.when((i == nz - 1) & (p > 0))
            def _():
                @pl.loop(0, 2)
                def _(h):
                    l_pass(1, h)

    @pl.loop(nz - lag, nz)
    def _(i):
        across_y(i)

    share(p)

    def l_pass_both(k):
        if k < far:

            @pl.when(p > 0)
            def _():
                @pl.loop(0, 2)
                def _(h):
                    l_pass(k, h)

    @pl.loop(0, nz - 1)
    def _(i):
        z_out[i] = across_z(i).astype(BF16)
        z_copy(i).start()

        if far > 2:

            @pl.when((i == nz // 2) & (p > 0))
            def _():
                @pl.loop(0, 2)
                def _(h):
                    l_pass(2, h)

    @pl.loop(0, p - 1)
    def _(m):
        share(m)

    def a_copy(d):
        to = (z + d) % nz
        return remote(act.at[p, z], act.at[p, z], a_s.at[d], a_r.at[p, z], p, col_of(to, y, c))

    def send_current():
        act[p, z] = res[...].astype(BF16)

        for d in far_first[:-1]:
            a_copy(d).start()

    def act_arrival(s, src):
        return remote(x_out, act.at[s, src], x_s.at[0, 0], a_r.at[s, src], p, col_of(src, y, c))

    def times(s, own_here):
        total = jnp.zeros((chunk, row_block), F32)
        for d in far_first[::-1]:
            src = (z + d) % nz
            if not (own_here and d == 0):
                act_arrival(s, src).wait_recv()
            columns = pl.ds(pl.multiple_of(src * row_block, row_block), row_block)
            total = total + dot_t(act[s, src], w[s, :, :, columns].reshape(row_block, row_block))
        return total

    for k in range(3, far):
        l_pass_both(k)

    @pl.when(p > 0)
    def _():
        forward(p)
        gathered(p)

        def columns_of(d):
            return pl.ds(pl.multiple_of(((z + d) % nz) * row_block, row_block), row_block)

        def part(d, block):
            return jnp.dot(
                w[p, :, :, columns_of(d)].reshape(row_block, row_block),
                block.reshape(row_block, row_block),
                preferred_element_type=F32,
            )

        macc[...] = jnp.zeros_like(macc)

        @pl.loop(1, nz + 1)
        def _(t):
            off = (t + far) % nz

            @pl.when((off == far) | ((off == far - 1) & (off > 0)))
            def _():
                @pl.loop(0, 2)
                def _(h):
                    l_arrival(off, h).wait_recv()

            macc[...] += part(off, lcol[(z + off) % nz])

        mw[g] = macc[...].astype(BF16)

        for d in y_near:
            m_y(d).start()

        m_c(y).start()

    own = across_z(nz - 1)
    for d in range(1, nz):
        z_arrival(d).wait_recv()
        own = own + z_in[(z + d) % nz].astype(F32)
    res[...] = -own

    @pl.when(p <= 1)
    def _():
        send_current()

    @pl.when(p == 0)
    def _():
        forward(p)

    @pl.when(p > 0)
    def _():
        @pl.loop(0, p - 1)
        def _(m):
            forward(m)

        for d in y_near:
            m_y_arrival(d).wait_recv()
            m_c((y + d) % ny).start()

        @pl.loop(0, p - 1)
        def _(s):
            gathered(s)
            res[...] -= times(s, False)

    @pl.when(p > 1)
    def _():
        send_current()

    @pl.when(p == 0)
    def _():
        gathered(p)

    def shared(m):
        @pl.loop(1, ny)
        def _(d):
            w_y(m, d).wait_send()

        @pl.loop(0, ny)
        def _(yy):
            w_c(m, yy).wait_send()

    shared(p)

    @pl.loop(0, p - 1)
    def _(m):
        shared(m)

    @pl.when(p > 0)
    def _():
        @pl.loop(1, group)
        def _(d):
            la_copy(d).wait_send()

        @pl.loop(0, 2)
        def _(h):
            @pl.loop(1, far + 1)
            def _(k):
                l_move(k, h, 0).wait_send()

            @pl.loop(1, far)
            def _(k):
                l_move(k, h, 1).wait_send()

    @pl.loop(0, nz)
    def _(i):
        core_copy(i).wait_send()

        @pl.loop(1, ny)
        def _(d):
            y_copy(i, d).wait_send()

    @pl.loop(0, nz - 1)
    def _(i):
        z_copy(i).wait_send()

    res[...] = times(p, True)

    @pl.when(p > 0)
    def _():
        @pl.loop(0, ny)
        def _(yy):
            m_c_arrival(yy).wait_recv()

        total = jnp.zeros((chunk, row_block), F32)
        for d in far_first[::-1]:
            src = (z + d) % nz
            act_arrival(last, src).wait_recv()
            total = total + dot_t(act[last, src], mw[src])
        res[...] -= total

    solved = res[...]
    x_out[...] = solved.astype(BF16)

    def x_copy(q, d):
        to = (z + d) % nz
        return remote(x_out, act.at[p, z], x_s.at[q, d], a_r.at[p, z], q, col_of(to, y, c))

    @pl.loop(0, np_ - 1 - p)
    def _(i):
        q = jnp.where(p == 0, 1 + i, np_ - 1 - i)
        pl.semaphore_wait(ready.at[q], 1)
        for d in far_first:
            x_copy(q, d).start()

    place[:half, :row_block] = jnp.zeros((half, row_block), F32)
    place[pl.ds(pl.multiple_of(y * chunk, chunk), chunk), :row_block] = solved
    final_out[...] = place[:half, :row_block].T.reshape(group, rows, half)

    def f_copy(d):
        to = (g + d) % group
        return remote(final_out.at[to], final_in.at[g], f_s.at[d], f_r.at[g], p, z * group + to)

    def f_arrival(d):
        src = (g + d) % group
        return remote(final_out.at[src], final_in.at[src], f_s.at[d], f_r.at[src], p, z * group + src)

    @pl.loop(1, group)
    def _(d):
        f_copy(d).start()

    final_in[g] = final_out[g]

    @pl.loop(1, group)
    def _(d):
        f_arrival(d).wait_recv()

    for cc in range(2):
        total = final_in[cc]
        for yy in range(1, ny):
            total = total + final_in[yy * 2 + cc]
        out_ref[:, cc * half : (cc + 1) * half] = total

    @pl.when(p > 0)
    def _():
        @pl.loop(1, ny)
        def _(d):
            m_y(d).wait_send()

        @pl.loop(0, ny)
        def _(yy):
            m_c(yy).wait_send()

    @pl.loop(1, nz)
    def _(d):
        a_copy(d).wait_send()

    @pl.loop(p + 1, np_)
    def _(q):
        @pl.loop(0, nz)
        def _(d):
            x_copy(q, d).wait_send()

    @pl.loop(1, group)
    def _(d):
        f_copy(d).wait_send()


def local(np_, nz, ny, right_side, prior_solution, factor_codes, block_scale, diag_inverse, inner_factor):
    rows, rhs = right_side.shape
    depth = prior_solution.shape[0]
    group = ny * 2
    row_block = rows * group
    half = rhs // 2
    chunk = half // ny
    width = diag_inverse.shape[-1]
    dma = pltpu.SemaphoreType.DMA
    scratch = [
        pltpu.VMEM((rows, rhs), F32),
        pltpu.SMEM(block_scale.shape, F32),
        pltpu.VMEM((depth, rhs), BF16),
        pltpu.VMEM((nz, row_block, depth), BF16),
        pltpu.VMEM((rhs, depth), BF16),
        pltpu.VMEM((row_block, rhs), F32),
        pltpu.VMEM((2, half, row_block), F32),
        pltpu.VMEM((nz, half, row_block), BF16),
        pltpu.VMEM((nz, half, row_block), BF16),
        pltpu.VMEM((nz, ny, chunk, row_block), F32),
        pltpu.VMEM((nz, ny, chunk, row_block), BF16),
        pltpu.VMEM((nz, ny, chunk, row_block), BF16),
        pltpu.VMEM((nz, chunk, row_block), BF16),
        pltpu.VMEM((nz, chunk, row_block), BF16),
        pltpu.VMEM((np_, group, rows, width), BF16),
        pltpu.VMEM((nz, group, rows, row_block), BF16),
        pltpu.VMEM((row_block, row_block), F32),
        pltpu.VMEM((group, row_block, row_block), BF16),
        pltpu.VMEM((np_, nz, chunk, row_block), BF16),
        pltpu.VMEM((chunk, row_block), BF16),
        pltpu.VMEM((chunk, row_block), F32),
        pltpu.VMEM((group, rows, half), F32),
        pltpu.VMEM((group, rows, half), F32),
        dma((3,)),
        dma((nz,)),
        dma((np_,)),
        dma((np_, ny)),
        dma((np_, ny)),
        dma((np_, ny)),
        dma((np_, ny)),
        dma((group,)),
        dma((group,)),
        dma((2, nz // 2, 2)),
        dma((nz, 2)),
        dma((ny,)),
        dma((ny,)),
        dma((ny,)),
        dma((ny,)),
        dma((nz,)),
        dma((nz,)),
        dma((nz, ny)),
        dma((nz, ny)),
        dma((nz,)),
        dma((nz,)),
        dma((nz,)),
        dma((np_, nz)),
        dma((np_, nz)),
        dma((group,)),
        dma((group,)),
        pltpu.SemaphoreType.REGULAR((np_,)),
    ]
    anywhere = pl.BlockSpec(memory_space=pl.ANY)
    return pl.pallas_call(
        functools.partial(kernel, np_, nz, ny),
        out_shape=jax.ShapeDtypeStruct((rows, rhs), F32),
        in_specs=[anywhere] * 6,
        out_specs=pl.BlockSpec(memory_space=pltpu.VMEM),
        scratch_shapes=scratch,
        compiler_params=pltpu.CompilerParams(collective_id=0, has_side_effects=True, vmem_limit_bytes=54 * 2**20 - 2**17),
        cost_estimate=pl.CostEstimate(
            flops=2 * nz * row_block * depth * rhs, bytes_accessed=2 * nz * row_block * depth, transcendentals=0
        ),
    )(right_side, prior_solution, factor_codes, block_scale, diag_inverse, inner_factor)


def build(mesh, ny):
    np_ = mesh.shape["row"]
    nz = mesh.shape["col"] // (2 * ny)
    return jax.shard_map(
        functools.partial(local, np_, nz, ny),
        mesh=mesh,
        in_specs=(
            P(("row", "col"), None),
            P("col", None),
            P("row", "col"),
            P("row", "col"),
            P("row", "col", None),
            P("row", None, "col", None),
        ),
        out_specs=P(("row", "col"), None),
        check_vma=False,
    )


def solution(mesh):
    return build(mesh, 4)
```
